256 devices in a mesh: tile: 32 (over z, x), round: 8 (over y, core).
Axes of the slice: x: 4, y: 4, z: 8, core: 2. Of those that a mesh axis runs over, the one named last changes fastest.
Arguments:
- images: bfloat16 [48, 2, 256, 8192], P('round', None, 'tile'), may hold values from 0.5 to 8
- labels: int32 [2, 256, 8192], P(None, 'round', 'tile'), may hold values from 0 to 256
- counts: int32 [32], replicated, may hold values from 64 to 256, as said below
- owners: int32 [8192, 1], P('tile'), may hold values from 0 to 31; in each aligned block of 256 rows (0 to 255, 256 to 511, ...) at most 16 rows name the same one
- codebook: bfloat16 [48, 550], replicated
Outputs:
- cell_genes: float32 [32, 32, 16, 550], P('tile')
The draws below stay inside these ranges and needn't reach their ends.
Inputs may be any that keep to these rules, and one draw needn't show every extreme that they name: `counts`: some tile has 256 live slots, and at least a quarter of them in every tile. `owners`: at most 16 slots of one tile have the same owner, and this is reached.
All inputs are finite; a program needn't handle non-finite values.
Results may differ from the reference program's by a relative error of at most 0.0027.
The reference program's roundings to bfloat16 on the way (of `unit` and `posterior`) count: a program that leaves them out, or rounds other values in their place, can miss the bound.
Values may be sent and summed in bfloat16 or wider, within the bound.
No kernel may reach another device: no remote copies, remote signals or barrier semaphores. Data moves between devices by JAX's collectives and lax.ppermute only.
A program may use at most 128 MiB of HBM per device.

```python
import math
import jax
import jax.numpy as jnp
import numpy as np
from jax import lax

CH = 48
GENES = 550
ZP = 2
PT = 256
CELL_TILE = 256
TILES = 32
NY = 256
NX = 8192
NCELLS = 8192
CAP = 16


def draw_counts(key, part):
    key = jax.random.fold_in(key, 7)
    first, second_half = jax.random.split(key)
    values = jax.random.randint(first, (TILES,), CELL_TILE // 4, CELL_TILE + 1)
    full_tile = jax.random.randint(second_half, (), 0, TILES)
    return jnp.where(jnp.arange(TILES) == full_tile, CELL_TILE, values).astype(jnp.int32)


def draw_codebook(key, part):
    key = jax.random.fold_in(key, 11)
    first = jax.random.fold_in(key, 0)
    base = jax.random.normal(first, (CH, GENES), jnp.float32)
    return base.astype(jnp.bfloat16)


def set_ends(entries, stream_key, low, largest):
    place = [jax.random.randint(jax.random.fold_in(stream_key, axis), (), 0, length) for axis, length in enumerate(entries.shape)]
    widest = entries.shape.index(max(entries.shape))
    beside = place[:widest] + [(place[widest] + 1) % entries.shape[widest]] + place[widest + 1:]
    return entries.at[tuple(place)].set(low).at[tuple(beside)].set(largest)


def levels(stream_key, shape, shards, least, top_value):
    gain, own = 1.0, jax.random.fold_in(stream_key, 6)
    for axis_at, shards_of in shards:
        heights = jnp.exp(jax.random.uniform(jax.random.fold_in(own, axis_at), (shards_of,), jnp.float32, least / len(shards), top_value / len(shards)))
        gain = gain * jnp.repeat(heights, shape[axis_at] // shards_of).reshape([-1 if axis == axis_at else 1 for axis in range(len(shape))])
    return gain


def assign_block(rng, own, number, rows, amount, top, most, slope):
    ranking = jax.random.permutation(rng, amount)
    heavy_load, usual = portions_of(amount, rows * top, most, slope, True), portions_of(amount, rows * top, most, slope, False)
    places = jnp.arange(amount)

    def named(tallies, turn):
        used = int((tallies > 0).sum())
        fixed = max(1, used // 4)
        moved = fixed + (places - fixed + turn * (used - fixed)) % max(1, amount - fixed)
        return jnp.zeros((amount,), jnp.int32).at[ranking[jnp.where(places < fixed, places, moved)]].set(jnp.asarray(tallies, jnp.int32))

    tallies = jnp.where(number % 4 == 0, named(heavy_load, number // 4), named(usual, number - number // 4 - 1))
    mixed = jax.random.permutation(jax.random.fold_in(own, 3), amount)
    giver, receiver = mixed[0:amount // 2 * 2:2], mixed[1:amount // 2 * 2:2]
    slack = jnp.minimum(tallies[giver] - 1, most - tallies[receiver]) // 2
    slack = jnp.where((giver == ranking[0]) | (receiver == ranking[0]) | (tallies[receiver] == 0), 0, jnp.maximum(slack, 0))
    moved = jax.random.randint(jax.random.fold_in(own, 4), (amount // 2,), 0, 1 << 20) % (slack + 1)
    tallies = tallies.at[giver].add(-moved).at[receiver].add(moved)
    members = jnp.searchsorted(jnp.cumsum(tallies), jnp.arange(rows * top), side="right").astype(jnp.int32)
    table = members.reshape(top, rows).T
    table = table[jax.random.permutation(jax.random.fold_in(own, 1), rows)]
    turn = jax.random.randint(jax.random.fold_in(own, 2), (rows, 1), 0, top)
    return jnp.take_along_axis(table, (jnp.arange(top)[None, :] + turn) % top, axis=1)


def portions_of(count, total, reach, slope, full):
    weights = [(1 << 20) // math.isqrt(rank ** slope) + 1 for rank in range(1, count + 1)]
    largest = reach if full else min(reach, max(-(-total // count), total * weights[0] // sum(weights)))
    least = 1 if total - largest >= count - 1 else 0
    given, surplus = [largest] + [least] * (count - 1), total - largest - least * (count - 1)
    while surplus > 0:
        candidates = [i for i in range(1, count) if given[i] < largest] or [i for i in range(1, count) if given[i] < reach]
        mass, remaining = sum([weights[i] for i in candidates]), surplus
        for i in candidates:
            more = min(reach - given[i], max(1, remaining * weights[i] // mass), surplus)
            given[i] = given[i] + more
            surplus = surplus - more
    return np.array(given)


def setup_inputs(seed: int = 0) -> dict:
    arg_keys = jax.random.split(jax.random.key(seed), 6)
    images = jnp.clip(jnp.exp(math.log(8.0) - 2.7725887 * jax.random.uniform(arg_keys[0], (CH, ZP, NY, NX), jnp.float32) ** levels(arg_keys[0], (CH, ZP, NY, NX), ((0, 8), (2, 32)), -0.2, 0.2)), 0.5, 8.0).astype(jnp.bfloat16)
    labels = set_ends(jax.random.randint(arg_keys[1], (ZP, NY, NX), 0, CELL_TILE + 1), jax.random.fold_in(arg_keys[1], 1), 0, CELL_TILE).astype(jnp.int32)
    counts = draw_counts(jax.random.fold_in(arg_keys[5], 71), 0)
    owners_keys = jax.random.split(jax.random.fold_in(arg_keys[3], 1), NCELLS // CELL_TILE)
    owners_turns = jax.random.permutation(jax.random.fold_in(arg_keys[3], 3), NCELLS // CELL_TILE)
    owners = jax.vmap(lambda own, number: assign_block(jax.random.fold_in(arg_keys[3], 2), own, number, CELL_TILE, TILES, 1, CAP, 1))(owners_keys, owners_turns).reshape((NCELLS, 1))
    codebook = draw_codebook(jax.random.fold_in(arg_keys[5], 71), 0)
    return {"images": images, "labels": labels, "counts": counts, "owners": owners, "codebook": codebook}


SOFTMAX_HEAT = 0.6
SHARPEN = 0.15
NOISE_LEVEL = 1.0

def stencil(padded_stack):
    zpadded = jnp.pad(padded_stack, ((0, 0), (1, 1), (0, 0), (0, 0)))
    center = padded_stack[:, :, 1:-1, 1:-1]
    beside = padded_stack[:, :, 2:, 1:-1] + padded_stack[:, :, :-2, 1:-1]
    beside = beside + padded_stack[:, :, 1:-1, 2:] + padded_stack[:, :, 1:-1, :-2]
    beside = beside + zpadded[:, 2:, 1:-1, 1:-1] + zpadded[:, :-2, 1:-1, 1:-1]
    return (center, beside)

def pad_plane(field):
    return jnp.pad(field, ((0, 0), (0, 0), (1, 1), (1, 1)))

def reference(images, labels, counts, owners, codebook):
    center, beside = stencil(pad_plane(images.astype(jnp.float32)))
    highpass = center - (center + beside) / 7.0
    center, beside = stencil(pad_plane(highpass))
    sharp = center + SHARPEN * (6.0 * center - beside)
    mean_square = lax.optimization_barrier(jnp.mean(sharp * sharp, axis=0))
    unit = (sharp / jnp.sqrt(mean_square + NOISE_LEVEL)).astype(jnp.bfloat16)

    def per_tile(tile_index):
        start = (tile_index * PT).astype(jnp.int32)
        tile_piece = lax.dynamic_slice_in_dim(unit, start, PT, 3).reshape(CH, -1)
        tile_labels = lax.dynamic_slice_in_dim(labels, start, PT, 2).reshape(-1)
        live = jnp.sum(jnp.where(jnp.arange(TILES) == tile_index, counts, 0))
        gene_logits = SOFTMAX_HEAT * jnp.dot(tile_piece.T, codebook, preferred_element_type=jnp.float32)
        posterior = jax.nn.softmax(gene_logits, axis=1).astype(jnp.bfloat16)
        segment = jnp.where(tile_labels < live, tile_labels, CELL_TILE)
        sums = jax.ops.segment_sum(posterior.astype(jnp.float32), segment, num_segments=CELL_TILE + 1)
        return sums[:CELL_TILE]
    cell_post = lax.map(per_tile, jnp.arange(TILES, dtype=jnp.int32))
    owner_of = owners[:, 0].reshape(TILES, CELL_TILE)
    chosen = (owner_of[:, :, None] == jnp.arange(TILES)[None, None, :]).astype(jnp.int32)
    before = jnp.cumsum(chosen, axis=1) - chosen
    slot = lax.optimization_barrier(jnp.sum(before * chosen, axis=2))
    source = jnp.broadcast_to(jnp.arange(TILES, dtype=jnp.int32)[:, None], (TILES, CELL_TILE))
    result = jnp.zeros((TILES, TILES, CAP, GENES), jnp.float32)
    return result.at[owner_of, source, slot].set(cell_post)
```

```python
import jax
import jax.numpy as jnp
from jax import lax
from jax.experimental import pallas as pl
from jax.experimental.pallas import tpu as pltpu
from jax.sharding import Mesh, PartitionSpec as P

SOFTMAX_HEAT = 0.6
SHARPEN = 0.15
NOISE_LEVEL = 1.0
LOG2E = 1.4426950408889634

CH, GENES, ZP, PT, CELLS, TILES, CAP = 48, 550, 2, 256, 256, 32, 16
NZ, NXD, NR = 8, 4, 8
GP = 552
COLOUR = CH // NR
PAIRS = COLOUR * ZP
PIECE = 2 * PAIRS + 1
ROWS = 32
SCALE = 0.25
F32, BF16 = jnp.float32, jnp.bfloat16


def pack_kernel(img, before, after, out):
    r = pl.program_id(0)
    lane = lax.broadcasted_iota(jnp.int32, (8, 128), 1)
    has_before, has_after = (r > 0).astype(F32), (r < NR - 1).astype(F32)
    for x in range(NXD):
        border = jnp.zeros((8, 128), F32)
        for i in range(PAIRS):
            c, p = i // ZP, i % ZP
            out[x, 0, 2 * i] = img[c, p, :, 256 * x : 256 * x + 128]
            out[x, 0, 2 * i + 1] = img[c, p, :, 256 * x + 128 : 256 * x + 256]
            if x < NXD - 1:
                right = img[c, p, :, 256 * x + 256 : 256 * x + 384].astype(F32)
            else:
                right = after[c, p].astype(F32) * has_after
            if x > 0:
                left = img[c, p, :, 256 * x - 128 : 256 * x].astype(F32)
            else:
                left = before[c, p].astype(F32) * has_before
            both = jnp.where(lane < 64, right, left)
            if i > 0:
                both = pltpu.roll(both, 4 * i, 1)
            border = jnp.where(((lane - 4 * i + 2) & 127) < 4, both, border)
        out[x, 0, 2 * PAIRS] = border.astype(BF16)


def pack(images):
    return pl.pallas_call(
        pack_kernel,
        grid=(NR,),
        in_specs=[
            pl.BlockSpec((COLOUR, ZP, 8, 1024), lambda r: (0, 0, 0, r)),
            pl.BlockSpec((COLOUR, ZP, 8, 128), lambda r: (0, 0, 0, jnp.maximum(8 * r - 1, 0))),
            pl.BlockSpec((COLOUR, ZP, 8, 128), lambda r: (0, 0, 0, jnp.minimum(8 * r + 8, 63))),
        ],
        out_specs=pl.BlockSpec((NXD, 1, PIECE, 8, 128), lambda r: (0, r, 0, 0, 0)),
        out_shape=jax.ShapeDtypeStruct((NXD, NR, PIECE, 8, 128), BF16),
        name="pack_pieces",
    )(images, images, images)


def neighbours(tiles, lane):
    n = len(tiles)
    up = [pltpu.roll(t, 1, 1) for t in tiles]
    down = [pltpu.roll(t, 127, 1) for t in tiles]
    first, last = lane == 0, lane == 127
    left = [jnp.where(first, up[k - 1], up[k]) for k in range(n)]
    right = [jnp.where(last, down[(k + 1) % n], down[k]) for k in range(n)]
    return left, right


def decode_kernel(g, gu, gd, labels, owners, counts, codebook, out, s, hp, unit, cbt, acc):
    z, x, r = lax.axis_index("z"), lax.axis_index("x"), lax.axis_index("r")
    tile = NXD * r + x
    lane = lax.broadcasted_iota(jnp.int32, (CH, 128), 1)

    def unpack(src, at, rr):
        border = src[2 * PAIRS].astype(F32)
        for i in range(PAIRS):
            c, p = i // ZP, i % ZP
            rows = pl.ds(pl.multiple_of((COLOUR * rr + c) * 8, 8), 8)
            s[0, at * ZP + p, rows, :] = src[2 * i].astype(F32)
            s[1, at * ZP + p, rows, :] = src[2 * i + 1].astype(F32)
            s[2, at * ZP + p, rows, :] = pltpu.roll(border, 128 - 4 * i, 1) if i else border

    def unpack_step(k, _):
        unpack(g.at[k], k // NR + 1, k % NR)
        return 0

    lax.fori_loop(0, NXD * NR, unpack_step, 0)

    def unpack_border(k, _):
        unpack(gu.at[k], 0, k)
        unpack(gd.at[k], NXD + 1, k)
        return 0

    lax.fori_loop(0, NR, unpack_border, 0)

    def raw(row, p):
        at, inner = (row + 8) // 8, (row + 8) % 8
        return [s[k, at * ZP + p, pl.ds(inner, CH, stride=8), :] for k in range(3)]

    left_ok = jnp.where(tile > 0, 1.0, 0.0)
    right_ok = jnp.where(tile < TILES - 1, 1.0, 0.0)
    edge = jnp.where(lane < 64, right_ok, left_ok)

    def highpass(k, _):
        row = k - 1
        inside = jnp.where(((row >= 0) | (z > 0)) & ((row < ROWS) | (z < NZ - 1)), 1.0, 0.0)
        mid = [raw(row, p) for p in range(ZP)]
        for p in range(ZP):
            above, below = raw(row - 1, p), raw(row + 1, p)
            left, right = neighbours(mid[p], lane)
            for t in range(3):
                beside = (below[t] + above[t]) + (right[t] + left[t]) + mid[1 - p][t]
                high = mid[p][t] - (mid[p][t] + beside) * (1.0 / 7.0)
                high = high * (edge * inside if t == 2 else inside)
                hp[k, p, t] = high
        return 0

    lax.fori_loop(0, ROWS + 2, highpass, 0)

    def sharpen(k, _):
        mid = [[hp[k + 1, p, t] for t in range(3)] for p in range(ZP)]
        for p in range(ZP):
            left, right = neighbours(mid[p], lane)
            for t in range(2):
                beside = (hp[k + 2, p, t] + hp[k, p, t]) + (right[t] + left[t]) + mid[1 - p][t]
                sharp = mid[p][t] + SHARPEN * (6.0 * mid[p][t] - beside)
                mean = jnp.sum(sharp * sharp, axis=0, keepdims=True) * (1.0 / CH)
                scaled = sharp * lax.rsqrt(mean + NOISE_LEVEL)
                unit[k, :, p * 256 + t * 128 : p * 256 + (t + 1) * 128] = scaled.astype(BF16)
        return 0

    lax.fori_loop(0, ROWS, sharpen, 0)

    wide = codebook[...].astype(F32) * (SOFTMAX_HEAT * LOG2E)
    flat = jnp.concatenate([wide, jnp.zeros((CH, GP - GENES), F32)], axis=1).T
    hi = flat.astype(BF16)
    mid = (flat - hi.astype(F32)).astype(BF16)
    lo = (flat - hi.astype(F32) - mid.astype(F32)).astype(BF16)
    gene = lax.broadcasted_iota(jnp.int32, (GP, 16), 0)
    which = lax.broadcasted_iota(jnp.int32, (GP, 16), 1)
    shut = jnp.where((gene >= GENES) & (which == 0), -3.0e38, 0.0).astype(BF16)
    cbt[...] = jnp.concatenate([hi, mid, lo, shut], axis=1)
    acc[...] = jnp.zeros_like(acc)
    slots = lax.broadcasted_iota(jnp.int32, (CELLS, ZP * PT), 0)

    def posterior(k, _):
        u = unit[k]
        stacked = jnp.concatenate([u, u, u, jnp.ones((16, ZP * PT), BF16)], axis=0)
        logits = jnp.dot(cbt[...], stacked, preferred_element_type=F32)
        top = jnp.max(logits, axis=0, keepdims=True)
        e = jnp.exp2(logits - top)
        total = jnp.sum(e, axis=0, keepdims=True)
        post = (e * (1.0 / total)).astype(BF16)
        row = jnp.concatenate([labels[p, pl.ds(k, 1), :] for p in range(ZP)], axis=1)
        onehot = jnp.where(slots == row, 1.0, 0.0).astype(BF16)
        acc[...] += lax.dot_general(post, onehot, (((1,), (1,)), ((), ())), preferred_element_type=F32)
        return 0

    lax.fori_loop(0, ROWS, posterior, 0)

    owner = owners[...]
    own = lax.broadcasted_iota(jnp.int32, (TILES, CELLS), 0) == owner
    own_f = jnp.where(own, 1.0, 0.0)
    earlier = lax.broadcasted_iota(jnp.int32, (CELLS, CELLS), 0) < lax.broadcasted_iota(jnp.int32, (CELLS, CELLS), 1)
    before = jnp.dot(own_f.astype(BF16), jnp.where(earlier, 1.0, 0.0).astype(BF16), preferred_element_type=F32)
    place = jnp.sum(own_f * before, axis=0, keepdims=True).astype(jnp.int32)
    cell = lax.broadcasted_iota(jnp.int32, (1, CELLS), 1)
    goes = jnp.where(cell < counts[tile], owner * CAP + place, -1)
    select = jnp.where(lax.broadcasted_iota(jnp.int32, (TILES * CAP, CELLS), 0) == goes, SCALE, 0.0).astype(BF16)
    sums = acc[...]
    high = sums.astype(BF16)
    low = (sums - high.astype(F32)).astype(BF16)
    nt = (((1,), (1,)), ((), ()))
    packed = lax.dot_general(select, high, nt, preferred_element_type=F32)
    packed = packed + lax.dot_general(select, low, nt, preferred_element_type=F32)
    out[...] = packed[:, :GENES]


def decode(g, gu, gd, labels, owners, counts, codebook):
    vmem, smem = pl.BlockSpec(memory_space=pltpu.VMEM), pl.BlockSpec(memory_space=pltpu.SMEM)
    return pl.pallas_call(
        decode_kernel,
        in_specs=[vmem, vmem, vmem, vmem, vmem, smem, vmem],
        out_specs=vmem,
        out_shape=jax.ShapeDtypeStruct((TILES * CAP, GENES), F32),
        scratch_shapes=[
            pltpu.VMEM((3, (NXD + 2) * ZP, CH * 8, 128), F32),
            pltpu.VMEM((ROWS + 2, ZP, 3, CH, 128), F32),
            pltpu.VMEM((ROWS, CH, ZP * PT), BF16),
            pltpu.VMEM((GP, 3 * CH + 16), BF16),
            pltpu.VMEM((GP, CELLS), F32),
        ],
        compiler_params=pltpu.CompilerParams(vmem_limit_bytes=48 * 1024 * 1024),
        name="decode_band",
    )(g, gu, gd, labels, owners, counts, codebook)


def local(images, labels, counts, owners, codebook):
    swap = [
        (z * NXD * NR + x * NR + r, r * NXD * NR + x * NR + z)
        for z in range(NZ)
        for x in range(NXD)
        for r in range(NR)
    ]
    everywhere = ("z", "x", "r")
    labels = lax.ppermute(labels, everywhere, swap)
    owners = lax.ppermute(owners.reshape(1, CELLS), everywhere, swap)
    pieces = pack(images).reshape(NXD * NR, PIECE, 8, 128)
    g = lax.all_to_all(pieces, ("x", "r"), split_axis=0, concat_axis=0, tiled=True)
    gu = lax.ppermute(g[(NXD - 1) * NR :], "z", [(i, i + 1) for i in range(NZ - 1)])
    gd = lax.ppermute(g[:NR], "z", [(i + 1, i) for i in range(NZ - 1)])
    packed = decode(g, gu, gd, labels, owners, counts, codebook)
    packed = packed.astype(jnp.float16).reshape(NZ, NXD * CAP, GENES)
    parts = lax.all_to_all(packed, "z", split_axis=0, concat_axis=0, tiled=True)
    summed = jnp.sum(parts.astype(F32), axis=0).astype(jnp.float16).reshape(NXD, 1, CAP, GENES)
    spread = jnp.broadcast_to(summed, (NXD, NR, CAP, GENES)).reshape(NXD * NR, CAP, GENES)
    received = lax.all_to_all(spread, ("x", "r"), split_axis=0, concat_axis=0, tiled=True)
    received = received.reshape(NXD, NR, CAP, GENES).transpose(1, 0, 2, 3).reshape(1, TILES, CAP, GENES)
    return received.astype(F32) * (1.0 / SCALE)


def solution(mesh):
    grid = Mesh(mesh.devices.reshape(NZ, NXD, NR), ("z", "x", "r"))
    in_specs = (P("r", None, ("z", "x"), None), P(None, "r", ("z", "x")), P(), P(("z", "x"), None), P())
    out_specs = P(("z", "x"), None, None, None)
    return jax.shard_map(local, mesh=grid, in_specs=in_specs, out_specs=out_specs, check_vma=False)
```

```python
import jax
import jax.numpy as jnp
from jax import lax
from jax.experimental import pallas as pl
from jax.experimental.pallas import tpu as pltpu
from jax.sharding import Mesh, PartitionSpec as P

SOFTMAX_HEAT = 0.6
SHARPEN = 0.15
NOISE_LEVEL = 1.0
LOG2E = 1.4426950408889634

CH, GENES, ZP, PT, CELLS, TILES, CAP = 48, 550, 2, 256, 256, 32, 16
NZ, NXD, NR = 8, 4, 8
GP = 552
COLOUR = CH // NR
PAIRS = COLOUR * ZP
PIECE = 2 * PAIRS + 1
ROWS = 32
WIDE = PT + 128
VOX = ZP * PT
SCALE = 0.25
SAFE = 100.0
F32, BF16 = jnp.float32, jnp.bfloat16
NT = (((1,), (1,)), ((), ()))


def position():
    return lax.axis_index("z"), lax.axis_index("x"), lax.axis_index("r")


def pack_kernel(img, labels, owners, counts, out, marks):
    z, x_here, _ = position()
    lane = lax.broadcasted_iota(jnp.int32, (8, 128), 1)
    windows = [(lane // 4) == i for i in range(PAIRS)]

    def column(r, _):
        start = pl.multiple_of(r * (NXD * PT), NXD * PT)
        before = pl.multiple_of(jnp.maximum(start - 128, 0), 128)
        after = pl.multiple_of(jnp.minimum(start + NXD * PT, (TILES * PT) - 128), 128)
        has_before, has_after = (r > 0).astype(F32), (r < NR - 1).astype(F32)
        for x in range(NXD):
            border = jnp.zeros((8, 128), F32)
            for i in range(PAIRS):
                c, p = i // ZP, i % ZP
                for t in range(2):
                    out[x * NR + r, 2 * i + t] = img[c, p, :, pl.ds(start + PT * x + 128 * t, 128)]
                if x < NXD - 1:
                    right = img[c, p, :, pl.ds(start + PT * (x + 1), 128)].astype(F32)
                else:
                    right = img[c, p, :, pl.ds(after, 128)].astype(F32) * has_after
                if x > 0:
                    left = img[c, p, :, pl.ds(start + PT * x - 128, 128)].astype(F32)
                else:
                    left = img[c, p, :, pl.ds(before, 128)].astype(F32) * has_before
                both = pltpu.roll(jnp.where(lane < 64, right, left), 4 * i + 2, 1)
                border = jnp.where(windows[i], both, border)
            out[x * NR + r, 2 * PAIRS] = border.astype(BF16)
        return 0

    lax.fori_loop(0, NR, column, 0)

    owner = owners[...]
    own = lax.broadcasted_iota(jnp.int32, (TILES, CELLS), 0) == owner
    own_f = jnp.where(own, 1.0, 0.0)
    earlier = lax.broadcasted_iota(jnp.int32, (CELLS, CELLS), 0) < lax.broadcasted_iota(jnp.int32, (CELLS, CELLS), 1)
    earlier = jnp.where(earlier, 1.0, 0.0).astype(BF16)
    ahead = jnp.dot(own_f.astype(BF16), earlier, preferred_element_type=F32)
    place = jnp.sum(own_f * ahead, axis=0, keepdims=True).astype(jnp.int32)
    cell = lax.broadcasted_iota(jnp.int32, (1, CELLS), 1)
    goes = jnp.where(cell < counts[NXD * z + x_here], owner * CAP + place, -1)
    for p in range(ZP):
        marks[p * ROWS : (p + 1) * ROWS] = labels[p]
    marks[ZP * ROWS :] = jnp.broadcast_to(goes, (8, CELLS))


def pack(images, labels, owners, counts):
    vmem, smem = pl.BlockSpec(memory_space=pltpu.VMEM), pl.BlockSpec(memory_space=pltpu.SMEM)
    return pl.pallas_call(
        pack_kernel,
        in_specs=[vmem, vmem, vmem, smem],
        out_specs=[vmem, vmem],
        out_shape=[
            jax.ShapeDtypeStruct((NXD * NR, PIECE, 8, 128), BF16),
            jax.ShapeDtypeStruct((ZP * ROWS + 8, CELLS), jnp.int32),
        ],
        compiler_params=pltpu.CompilerParams(vmem_limit_bytes=32 * 1024 * 1024),
        name="pack_pieces",
    )(images, labels, owners, counts)


def channels_last(load):
    return [jnp.swapaxes(jnp.stack([load(r, c) for r in range(NR)]).astype(F32), 0, 1) for c in range(COLOUR)]


def border_masks():
    lane = lax.broadcasted_iota(jnp.int32, (CH, 128), 1)
    colour = lax.broadcasted_iota(jnp.int32, (CH, 128), 0) // NR
    return [(lane // 4) == colour * ZP + p for p in range(ZP)]


def transposed_rows(src, rows, store):
    masks = border_masks()
    edge = jnp.swapaxes(jnp.stack([src(r, 2 * PAIRS) for r in range(NR)]).astype(F32), 0, 1)
    for p in range(ZP):
        for t in range(2):
            parts = channels_last(lambda r, c: src(r, 2 * (ZP * c + p) + t))
            for row in rows:
                block = jnp.concatenate([part[row] for part in parts], axis=0)
                store(row, p, t, block.astype(BF16))
        for row in rows:
            block = jnp.concatenate([edge[row]] * COLOUR, axis=0)
            store(row, p, 2, jnp.where(masks[p], block, 0.0).astype(BF16))


def stencil_kernel(g, unit, rim, ends, band, xt, y, a_s, b_s):
    z, x, r = position()
    tile = NXD * r + x
    left_ok = (tile > 0).astype(F32)
    right_ok = (tile < TILES - 1).astype(F32)

    source = lax.broadcasted_iota(jnp.int32, (WIDE, PT), 0)
    target = lax.broadcasted_iota(jnp.int32, (WIDE, PT), 1)
    e = source - PT
    side = e % 4
    beyond = jnp.where(side < 2, side - 2, PT - 2 + side)
    at = jnp.where(source < PT, source, jnp.where(e < 4 * PAIRS, beyond, 4 * WIDE))
    gap = jnp.abs(at - target)
    own = 2.0 - jnp.where(at == 0, 1.0 - left_ok, 0.0) - jnp.where(at == PT - 1, 1.0 - right_ok, 0.0)
    band[:, :PT] = jnp.where(gap == 1, 1.0, 0.0).astype(BF16)
    band[:, PT:] = jnp.where(gap == 2, 1.0, jnp.where(gap == 0, own, 0.0)).astype(BF16)

    step = ZP * CH
    blank = jnp.zeros((step, WIDE), BF16)
    xt[:step] = blank
    xt[(ROWS + 1) * step :] = blank

    def regroup(k, _):
        base = (k * 8 + 1) * step

        def store(row, p, t, block):
            start = pl.multiple_of(base + (row * ZP + p) * CH, 16)
            xt[pl.ds(start, CH), t * 128 : (t + 1) * 128] = block

        transposed_rows(lambda r, i: g[k * NR + r, i], range(8), store)
        rows = xt[pl.ds(pl.multiple_of(base, 16), 8 * step), :]
        y[pl.ds(pl.multiple_of(k * 8 * step, 16), 8 * step), :] = jnp.dot(rows, band[...], preferred_element_type=F32)
        return 0

    lax.fori_loop(0, ROWS // 8, regroup, 0)

    def raw(row, p, t):
        start = pl.multiple_of((row + 1) * step + p * CH, 16)
        return xt[pl.ds(start, CH), t * 128 : (t + 1) * 128].astype(F32)

    def cols(row, p, t, twice):
        start = pl.multiple_of(row * step + p * CH, 16)
        at = twice * PT + t * 128
        return y[pl.ds(start, CH), at : at + 128]

    b_s[0] = jnp.zeros_like(b_s[0])
    b_s[ROWS + 1] = jnp.zeros_like(b_s[0])

    def first(row, _):
        for t in range(2):
            here = [raw(row, p, t) for p in range(ZP)]
            for p in range(ZP):
                mx = 6.0 * here[p] - (raw(row - 1, p, t) + raw(row + 1, p, t)) - here[1 - p]
                cx = cols(row, p, t, 0)
                a = mx - cx
                a_s[row, p, t] = a
                b_s[row + 1, p, t] = a - cx
        return 0

    lax.fori_loop(0, ROWS, first, 0)

    def sharp7(row, t):
        mid = [b_s[row + 1, p, t] for p in range(ZP)]
        outs = []
        for p in range(ZP):
            mb = 6.0 * mid[p] - (b_s[row, p, t] + b_s[row + 2, p, t]) - mid[1 - p]
            outs.append(a_s[row, p, t] + SHARPEN * (mb + cols(row, p, t, 1)))
        return outs

    def second(row, _):
        for t in range(2):
            for p, value in enumerate(sharp7(row, t)):
                unit[row, :, p * PT + t * 128 : p * PT + (t + 1) * 128] = normalise(value)
        return 0

    lax.fori_loop(2, ROWS - 2, second, 0)
    for k, row in enumerate((0, 1, ROWS - 2, ROWS - 1)):
        for t in range(2):
            for p, value in enumerate(sharp7(row, t)):
                rim[k, p, t] = value
    for k, row in enumerate((0, ROWS - 1)):
        for t in range(2):
            for p in range(ZP):
                ends[k, p, t] = raw(row, p, t)


def normalise(value):
    mean = jnp.sum(value * value, axis=0, keepdims=True) * (1.0 / CH)
    return (value * lax.rsqrt(mean + 49.0 * NOISE_LEVEL)).astype(BF16)


def stencil(g):
    vmem = pl.BlockSpec(memory_space=pltpu.VMEM)
    step = ZP * CH
    return pl.pallas_call(
        stencil_kernel,
        in_specs=[vmem],
        out_specs=[vmem] * 4,
        out_shape=[
            jax.ShapeDtypeStruct((ROWS, CH, VOX), BF16),
            jax.ShapeDtypeStruct((4, ZP, 2, CH, 128), F32),
            jax.ShapeDtypeStruct((2, ZP, 2, CH, 128), F32),
            jax.ShapeDtypeStruct((WIDE, 2 * PT), BF16),
        ],
        scratch_shapes=[
            pltpu.VMEM(((ROWS + 2) * step, WIDE), BF16),
            pltpu.VMEM((ROWS * step, 2 * PT), F32),
            pltpu.VMEM((ROWS, ZP, 2, CH, 128), F32),
            pltpu.VMEM((ROWS + 2, ZP, 2, CH, 128), F32),
        ],
        compiler_params=pltpu.CompilerParams(vmem_limit_bytes=40 * 1024 * 1024),
        cost_estimate=pl.CostEstimate(flops=8_000_000_000, bytes_accessed=8_000_000, transcendentals=0),
        name="stencil_band",
    )(g)


def posterior_kernel(unit, rim, ends, band, gu, gd, marks, codebook, out, xh, ue, cbt, acc, e0, e1):
    z = position()[0]
    for side, src in enumerate((gu, gd)):
        near, far = (7, 6) if side == 0 else (0, 1)

        def store(row, p, t, block):
            start = (p + (0 if row == near else ZP)) * CH
            xh[start : start + CH, t * 128 : (t + 1) * 128] = block

        transposed_rows(lambda r, i: src[r, i], (near, far), store)
        cx = jnp.dot(xh[: ZP * CH], band[:, :PT], preferred_element_type=F32)
        inside = jnp.where((z > 0) if side == 0 else (z < NZ - 1), 1.0, 0.0)
        k0, k1 = (0, 1) if side == 0 else (3, 2)
        for t in range(2):
            lanes = slice(t * 128, (t + 1) * 128)
            x1 = [xh[p * CH : (p + 1) * CH, lanes].astype(F32) for p in range(ZP)]
            x2 = [xh[(p + ZP) * CH : (p + ZP + 1) * CH, lanes].astype(F32) for p in range(ZP)]
            for p in range(ZP):
                b1 = 6.0 * x1[p] - (ends[side, p, t] + x2[p]) - x1[1 - p] - 2.0 * cx[p * CH : (p + 1) * CH, lanes]
                b1 = b1 * inside
                at = slice(p * PT + t * 128, p * PT + (t + 1) * 128)
                ue[k0, :, at] = normalise(rim[k0, p, t] - x1[p] + SHARPEN * (x1[1 - p] - 6.0 * x1[p] - b1))
                ue[k1, :, at] = normalise(rim[k1, p, t] + SHARPEN * x1[p])

    out_row = lax.broadcasted_iota(jnp.int32, (CH, CH), 0)
    in_row = lax.broadcasted_iota(jnp.int32, (CH, CH), 1)
    order = jnp.where(in_row == (out_row % NR) * COLOUR + out_row // NR, 1.0, 0.0).astype(BF16)
    wide = jnp.dot(order, codebook[...], preferred_element_type=F32)
    bound = jnp.max(jnp.sum(wide * wide, axis=0, keepdims=True))
    fine = bound * (CH * (1.01 * SOFTMAX_HEAT * LOG2E) ** 2) <= SAFE * SAFE
    wide = wide * (SOFTMAX_HEAT * LOG2E)
    flat = jnp.concatenate([wide, jnp.zeros((CH, GP - GENES), F32)], axis=1).T
    hi = flat.astype(BF16)
    mid = (flat - hi.astype(F32)).astype(BF16)
    lo = (flat - hi.astype(F32) - mid.astype(F32)).astype(BF16)
    gene = lax.broadcasted_iota(jnp.int32, (GP, 16), 0)
    which = lax.broadcasted_iota(jnp.int32, (GP, 16), 1)
    shut = jnp.where((gene >= GENES) & (which == 0), -3.0e38, 0.0).astype(BF16)
    cbt[...] = jnp.concatenate([hi, mid, lo, shut], axis=1)
    acc[...] = jnp.zeros_like(acc)
    slots = lax.broadcasted_iota(jnp.int32, (CELLS, VOX), 0)
    rim_rows = (0, 1, ROWS - 2, ROWS - 1)

    def logits_of(u):
        stacked = jnp.concatenate([u, u, u, jnp.ones((16, VOX), BF16)], axis=0)
        return jnp.dot(cbt[...], stacked, preferred_element_type=F32)

    def add(post, row):
        label = jnp.concatenate([marks[pl.ds(p * ROWS + row, 1), :] for p in range(ZP)], axis=1)
        onehot = jnp.where(slots == label, 1.0, 0.0).astype(BF16)
        acc[...] += lax.dot_general(post, onehot, NT, preferred_element_type=F32)

    def plain(u, e_s):
        e = jnp.exp2(logits_of(u))
        e_s[...] = e
        return 1.0 / jnp.sum(e, axis=0, keepdims=True)

    def finish(inverse, row, e_s):
        add((e_s[...] * inverse).astype(BF16), row)

    @pl.when(fine)
    def _():
        inv = plain(ue[0], e0)
        nxt = plain(ue[1], e1)
        finish(inv, 0, e0)
        inv = plain(ue[2], e0)
        finish(nxt, 1, e1)
        nxt = plain(ue[3], e1)
        finish(inv, ROWS - 2, e0)
        inv = plain(unit[2], e0)
        finish(nxt, ROWS - 1, e1)

        def pair(k, inv):
            row = 2 * k + 2
            nxt = plain(unit[row + 1], e1)
            finish(inv, row, e0)
            inv = plain(unit[jnp.minimum(row + 2, ROWS - 3)], e0)
            finish(nxt, row + 1, e1)
            return inv

        lax.fori_loop(0, (ROWS - 4) // 2, pair, inv)

    @pl.when(jnp.logical_not(fine))
    def _():
        def careful(u, row):
            logits = logits_of(u)
            e = jnp.exp2(logits - jnp.max(logits, axis=0, keepdims=True))
            add((e * (1.0 / jnp.sum(e, axis=0, keepdims=True))).astype(BF16), row)

        def inner(row, _):
            careful(unit[row], row)
            return 0

        def outer(k, _):
            careful(ue[k], jnp.where(k < 2, k, ROWS - 4 + k))
            return 0

        lax.fori_loop(2, ROWS - 2, inner, 0)
        lax.fori_loop(0, 4, outer, 0)

    goes = marks[ZP * ROWS : ZP * ROWS + 1]
    select = jnp.where(lax.broadcasted_iota(jnp.int32, (TILES * CAP, CELLS), 0) == goes, SCALE, 0.0).astype(BF16)
    sums = acc[...]
    high = sums.astype(BF16)
    low = (sums - high.astype(F32)).astype(BF16)
    packed = lax.dot_general(select, high, NT, preferred_element_type=F32)
    packed = packed + lax.dot_general(select, low, NT, preferred_element_type=F32)
    out[...] = packed[:, :GENES]


def posterior(unit, rim, ends, band, gu, gd, marks, codebook):
    vmem = pl.BlockSpec(memory_space=pltpu.VMEM)
    return pl.pallas_call(
        posterior_kernel,
        in_specs=[vmem] * 8,
        out_specs=vmem,
        out_shape=jax.ShapeDtypeStruct((TILES * CAP, GENES), F32),
        scratch_shapes=[
            pltpu.VMEM((2 * ZP * CH, WIDE), BF16),
            pltpu.VMEM((4, CH, VOX), BF16),
            pltpu.VMEM((GP, 3 * CH + 16), BF16),
            pltpu.VMEM((GP, CELLS), F32),
            pltpu.VMEM((GP, VOX), F32),
            pltpu.VMEM((GP, VOX), F32),
        ],
        compiler_params=pltpu.CompilerParams(vmem_limit_bytes=40 * 1024 * 1024),
        name="posterior_sums",
    )(unit, rim, ends, band, gu, gd, marks, codebook)


def local(images, labels, counts, owners, codebook):
    swap = [
        (z * NXD * NR + x * NR + r, r * NXD * NR + x * NR + z)
        for z in range(NZ)
        for x in range(NXD)
        for r in range(NR)
    ]
    pieces, marks = pack(images, labels, owners.reshape(1, CELLS), counts)
    marks = lax.ppermute(marks, ("z", "x", "r"), swap)
    g = lax.all_to_all(pieces, ("x", "r"), split_axis=0, concat_axis=0, tiled=True)
    gu = lax.ppermute(g[(NXD - 1) * NR :], "z", [(i, i + 1) for i in range(NZ - 1)])
    gd = lax.ppermute(g[:NR], "z", [(i + 1, i) for i in range(NZ - 1)])
    unit, rim, ends, band = stencil(g)
    packed = posterior(unit, rim, ends, band, gu, gd, marks, codebook)
    packed = packed.astype(jnp.float16).reshape(NZ, NXD * CAP, GENES)
    parts = lax.all_to_all(packed, "z", split_axis=0, concat_axis=0, tiled=True)
    summed = jnp.sum(parts.astype(F32), axis=0).astype(jnp.float16).reshape(NXD, 1, CAP, GENES)
    spread = jnp.broadcast_to(summed, (NXD, NR, CAP, GENES)).reshape(NXD * NR, CAP, GENES)
    received = lax.all_to_all(spread, ("x", "r"), split_axis=0, concat_axis=0, tiled=True)
    received = received.reshape(NXD, NR, CAP, GENES).transpose(1, 0, 2, 3).reshape(1, TILES, CAP, GENES)
    return received.astype(F32) * (1.0 / SCALE)


def solution(mesh):
    grid = Mesh(mesh.devices.reshape(NZ, NXD, NR), ("z", "x", "r"))
    in_specs = (P("r", None, ("z", "x"), None), P(None, "r", ("z", "x")), P(), P(("z", "x"), None), P())
    out_specs = P(("z", "x"), None, None, None)
    return jax.shard_map(local, mesh=grid, in_specs=in_specs, out_specs=out_specs, check_vma=False)
```

```python
import functools

import jax
import jax.numpy as jnp
from jax import lax
from jax.experimental import pallas as pl
from jax.experimental.pallas import tpu as pltpu
from jax.sharding import Mesh, PartitionSpec as P

SOFTMAX_HEAT = 0.6
SHARPEN = 0.15
NOISE_LEVEL = 1.0
LOG2E = 1.4426950408889634

CH, GENES, ZP, PT, CELLS, TILES, CAP = 48, 550, 2, 256, 256, 32, 16
NZ, NXD, NR = 8, 4, 8
GP = 552
COLOUR = CH // NR
PAIRS = COLOUR * ZP
HALF = PT // 2
PIECE = PAIRS + 1
ROWS = 32
STEP = ZP * CH
WIDE = HALF + 128
VOX = 2 * ZP * HALF
MARKS = ZP * ROWS + 8
FULL = GENES // 128
REST = GENES - 128 * FULL
OUT_ROWS = FULL * CAP + CAP // 2
SCALE = 0.25
SAFE = 100.0
F32, BF16 = jnp.float32, jnp.bfloat16
NT = (((1,), (1,)), ((), ()))
VMEM = pl.BlockSpec(memory_space=pltpu.VMEM)
SMEM = pl.BlockSpec(memory_space=pltpu.SMEM)
MIB = 1024 * 1024


def position():
    return lax.axis_index("z"), lax.axis_index("x"), lax.axis_index("r")


def params(mib):
    return pltpu.CompilerParams(vmem_limit_bytes=mib * MIB)


def cost(us):
    return pl.CostEstimate(flops=int(us * 1e9), bytes_accessed=int(us * 3e6), transcendentals=0)


def pack_kernel(half, img, out, buf, sems):
    lane = lax.broadcasted_iota(jnp.int32, (8, 128), 1)
    windows = [(lane // 4) == i for i in range(PAIRS)]

    def fetch(r):
        start = pl.multiple_of(r * (NXD * PT), NXD * PT)
        return pltpu.make_async_copy(img.at[:, :, :, pl.ds(start, NXD * PT)], buf.at[r], sems.at[r])

    for r in range(NR):
        fetch(r).start()
    if half:
        fetch(0).wait()

    def column(r, _):
        if half:

            @pl.when(r < NR - 1)
            def _():
                fetch(jnp.minimum(r + 1, NR - 1)).wait()
        else:
            fetch(r).wait()
        near = jnp.minimum(r + 1, NR - 1) if half else jnp.maximum(r - 1, 0)
        inside = ((r < NR - 1) if half else (r > 0)).astype(F32)
        for x in range(NXD):
            at = PT * x + HALF * half
            border = jnp.zeros((8, 128), F32)
            for i in range(PAIRS):
                c, p = i // ZP, i % ZP
                out[x * NR + r, i] = buf[r, c, p, :, at : at + HALF]
                if at + HALF < NXD * PT:
                    right = buf[r, c, p, :, at + HALF : at + 2 * HALF].astype(F32)
                else:
                    right = buf[near, c, p, :, :128].astype(F32) * inside
                if at > 0:
                    left = buf[r, c, p, :, at - 128 : at].astype(F32)
                else:
                    left = buf[near, c, p, :, NXD * PT - 128 :].astype(F32) * inside
                both = pltpu.roll(jnp.where(lane < 64, right, left), 4 * i + 2, 1)
                border = jnp.where(windows[i], both, border)
            out[x * NR + r, PAIRS] = border.astype(BF16)
        return 0

    lax.fori_loop(0, NR, column, 0)


def pack(images, half):
    return pl.pallas_call(
        functools.partial(pack_kernel, half),
        in_specs=[pl.BlockSpec(memory_space=pltpu.HBM)],
        out_specs=VMEM,
        out_shape=jax.ShapeDtypeStruct((NXD * NR, PIECE, 8, 128), BF16),
        scratch_shapes=[pltpu.VMEM((NR, COLOUR, ZP, 8, NXD * PT), BF16), pltpu.SemaphoreType.DMA((NR,))],
        compiler_params=params(16),
        cost_estimate=cost(2),
        name="pack_half",
    )(images)


def prepare_kernel(labels, owners, counts, codebook, marks, cbt, bands):
    z, x, r = position()
    owner = owners[...]
    own = lax.broadcasted_iota(jnp.int32, (TILES, CELLS), 0) == owner
    own_f = jnp.where(own, 1.0, 0.0)
    earlier = lax.broadcasted_iota(jnp.int32, (CELLS, CELLS), 0) < lax.broadcasted_iota(jnp.int32, (CELLS, CELLS), 1)
    earlier = jnp.where(earlier, 1.0, 0.0).astype(BF16)
    ahead = jnp.dot(own_f.astype(BF16), earlier, preferred_element_type=F32)
    place = jnp.sum(own_f * ahead, axis=0, keepdims=True).astype(jnp.int32)
    cell = lax.broadcasted_iota(jnp.int32, (1, CELLS), 1)
    goes = jnp.where(cell < counts[NXD * z + x], owner * CAP + place, -1)
    for p in range(ZP):
        marks[p * ROWS : (p + 1) * ROWS] = labels[p]
    marks[ZP * ROWS :] = jnp.broadcast_to(goes, (8, CELLS))

    out_row = lax.broadcasted_iota(jnp.int32, (CH, CH), 0)
    in_row = lax.broadcasted_iota(jnp.int32, (CH, CH), 1)
    order = jnp.where(in_row == (out_row % NR) * COLOUR + out_row // NR, 1.0, 0.0).astype(BF16)
    wide = jnp.dot(order, codebook[...], preferred_element_type=F32) * (SOFTMAX_HEAT * LOG2E)
    flat = jnp.concatenate([wide, jnp.zeros((CH, GP - GENES), F32)], axis=1).T
    hi = flat.astype(BF16)
    mid = (flat - hi.astype(F32)).astype(BF16)
    lo = (flat - hi.astype(F32) - mid.astype(F32)).astype(BF16)
    gene = lax.broadcasted_iota(jnp.int32, (GP, 16), 0)
    which = lax.broadcasted_iota(jnp.int32, (GP, 16), 1)
    shut = jnp.where((gene >= GENES) & (which == 0), -3.0e38, 0.0).astype(BF16)
    cbt[...] = jnp.concatenate([hi, mid, lo, shut], axis=1)

    tile = NXD * r + x
    source = lax.broadcasted_iota(jnp.int32, (WIDE, HALF), 0)
    target = lax.broadcasted_iota(jnp.int32, (WIDE, HALF), 1)
    e = source - HALF
    side = e % 4
    beyond = jnp.where(side < 2, side - 2, HALF - 2 + side)
    at = jnp.where(source < HALF, source, jnp.where(e < 4 * PAIRS, beyond, 4 * WIDE))
    gap = jnp.abs(at - target)
    once = jnp.where(gap == 1, 1.0, 0.0).astype(BF16)
    for half in range(2):
        outer = (tile == TILES - 1) if half else (tile == 0)
        edge = jnp.where(at == (HALF - 1 if half else 0), jnp.where(outer, 1.0, 0.0), 0.0)
        bands[half, :, :HALF] = once
        bands[half, :, HALF:] = jnp.where(gap == 2, 1.0, jnp.where(gap == 0, 2.0 - edge, 0.0)).astype(BF16)


def prepare(labels, owners, counts, codebook):
    return pl.pallas_call(
        prepare_kernel,
        in_specs=[VMEM, VMEM, SMEM, VMEM],
        out_specs=[VMEM] * 3,
        out_shape=[
            jax.ShapeDtypeStruct((MARKS, CELLS), jnp.int32),
            jax.ShapeDtypeStruct((GP, 3 * CH + 16), BF16),
            jax.ShapeDtypeStruct((2, WIDE, 2 * HALF), BF16),
        ],
        compiler_params=params(16),
        cost_estimate=cost(2),
        name="prepare",
    )(labels, owners, counts, codebook)


def transposed_rows(src, rows, store):
    lane = lax.broadcasted_iota(jnp.int32, (CH, 128), 1)
    colour = lax.broadcasted_iota(jnp.int32, (CH, 128), 0) // NR

    def swapped(i):
        return jnp.swapaxes(jnp.stack([src(r, i) for r in range(NR)]).astype(F32), 0, 1)

    edge = swapped(PAIRS)
    for p in range(ZP):
        parts = [swapped(ZP * c + p) for c in range(COLOUR)]
        mask = (lane // 4) == colour * ZP + p
        for row in rows:
            store(row, p, 0, jnp.concatenate([part[row] for part in parts], axis=0).astype(BF16))
            border = jnp.concatenate([edge[row]] * COLOUR, axis=0)
            store(row, p, 1, jnp.where(mask, border, 0.0).astype(BF16))


def normalise(value):
    mean = jnp.sum(value * value, axis=0, keepdims=True) * (1.0 / CH)
    return (value * lax.rsqrt(mean + 49.0 * NOISE_LEVEL)).astype(BF16)


def vertical(first, second, third):
    return 6.0 * second - (first + third)


def stencil_kernel(half, g, bands, unit, last, xt, y, a_s, b_s):
    def regroup(k, _):
        base = k * 8 * STEP

        def store(row, p, t, block):
            start = pl.multiple_of(base + (row * ZP + p) * CH, 16)
            xt[pl.ds(start, CH), t * 128 : (t + 1) * 128] = block

        transposed_rows(lambda r, i: g[k * NR + r, i], range(8), store)
        at = pl.ds(pl.multiple_of(base, 16), 8 * STEP)
        y[at, :] = jnp.dot(xt[at, :], bands[half], preferred_element_type=F32)
        return 0

    lax.fori_loop(0, ROWS // 8, regroup, 0)
    last[...] = xt[(ROWS - 4) * STEP :]

    def raw(row, p):
        return xt[pl.ds(pl.multiple_of(row * STEP + p * CH, 16), CH), :HALF].astype(F32)

    def cols(row, p, twice):
        return y[pl.ds(pl.multiple_of(row * STEP + p * CH, 16), CH), twice * HALF : (twice + 1) * HALF]

    def first(row, _):
        here = [raw(row, p) for p in range(ZP)]
        for p in range(ZP):
            cx = cols(row, p, 0)
            a = vertical(raw(row - 1, p), here[p], raw(row + 1, p)) - here[1 - p] - cx
            a_s[row, p] = a
            b_s[row, p] = a - cx
        return 0

    lax.fori_loop(1, ROWS - 1, first, 0)

    def second(k, _):
        for odd in range(2):
            row = 2 * k + odd
            mid = [b_s[row, p] for p in range(ZP)]
            for p in range(ZP):
                mb = vertical(b_s[row - 1, p], mid[p], b_s[row + 1, p]) - mid[1 - p]
                at = (odd * ZP + p) * HALF
                unit[k, :, at : at + HALF] = normalise(a_s[row, p] + SHARPEN * (mb + cols(row, p, 1)))
        return 0

    lax.fori_loop(1, ROWS // 2 - 1, second, 0)


def stencil(g, bands, half):
    return pl.pallas_call(
        functools.partial(stencil_kernel, half),
        in_specs=[VMEM] * 2,
        out_specs=[VMEM] * 2,
        out_shape=[
            jax.ShapeDtypeStruct((ROWS // 2, CH, VOX), BF16),
            jax.ShapeDtypeStruct((4 * STEP, WIDE), BF16),
        ],
        scratch_shapes=[
            pltpu.VMEM((ROWS * STEP, WIDE), BF16),
            pltpu.VMEM((ROWS * STEP, 2 * HALF), F32),
            pltpu.VMEM((ROWS, ZP, CH, HALF), F32),
            pltpu.VMEM((ROWS, ZP, CH, HALF), F32),
        ],
        compiler_params=params(24),
        cost_estimate=cost(4),
        name="stencil_half",
    )(g, bands)


def no_maximum_needed(codebook):
    wide = codebook[...].astype(F32)
    longest = jnp.max(jnp.sum(wide * wide, axis=0, keepdims=True))
    return longest * (CH * (1.01 * SOFTMAX_HEAT * LOG2E) ** 2) <= SAFE * SAFE


def posteriors(fine, steps, take, mark, cbt, acc, e0, e1):
    slots = lax.broadcasted_iota(jnp.int32, (CELLS, VOX), 0)

    def logits_of(u):
        stacked = jnp.concatenate([u, u, u, jnp.ones((16, VOX), BF16)], axis=0)
        return jnp.dot(cbt[...], stacked, preferred_element_type=F32)

    def add(post, k):
        onehot = jnp.where(slots == mark(k), 1.0, 0.0).astype(BF16)
        acc[...] += lax.dot_general(post, onehot, NT, preferred_element_type=F32)

    def begin(k, e_s):
        e = jnp.exp2(logits_of(take(k)))
        e_s[...] = e
        return 1.0 / jnp.sum(e, axis=0, keepdims=True)

    def finish(inverse, k, e_s):
        add((e_s[...] * inverse).astype(BF16), k)

    @pl.when(fine)
    def _():
        def pair(k, inv):
            nxt = begin(2 * k + 1, e1)
            finish(inv, 2 * k, e0)
            inv = begin(2 * k + 2, e0)
            finish(nxt, 2 * k + 1, e1)
            return inv

        inv = lax.fori_loop(0, steps // 2 - 1, pair, begin(0, e0))
        nxt = begin(steps - 1, e1)
        finish(inv, steps - 2, e0)
        finish(nxt, steps - 1, e1)

    @pl.when(jnp.logical_not(fine))
    def _():
        def careful(k, _):
            logits = logits_of(take(k))
            e = jnp.exp2(logits - jnp.max(logits, axis=0, keepdims=True))
            add((e * (1.0 / jnp.sum(e, axis=0, keepdims=True))).astype(BF16), k)
            return 0

        lax.fori_loop(0, steps, careful, 0)


def label_row(marks, half, row):
    parts = [marks[pl.ds(p * ROWS + row + odd, 1), :] for odd in range(2) for p in range(ZP)]
    return jnp.concatenate([part[:, half * HALF : (half + 1) * HALF] for part in parts], axis=1)


def inner_kernel(half, unit, marks, cbt, codebook, *refs):
    if half:
        given, acc, e0, e1 = refs
        acc[...] = given[...]
    else:
        acc, tops, e0, e1 = refs
        acc[...] = jnp.zeros_like(acc)
        parts = [
            marks[p * ROWS + row : p * ROWS + row + 1, h * HALF : (h + 1) * HALF]
            for h in range(2)
            for row in range(2)
            for p in range(ZP)
        ]
        tops[...] = jnp.concatenate(parts, axis=0).astype(F32).astype(BF16)
    posteriors(
        no_maximum_needed(codebook),
        ROWS // 2 - 2,
        lambda k: unit[k + 1],
        lambda k: label_row(marks, half, 2 * k + 2),
        cbt, acc, e0, e1,
    )


def inner(unit, marks, cbt, codebook, half, *given):
    sums = jax.ShapeDtypeStruct((GP, CELLS), F32)
    return pl.pallas_call(
        functools.partial(inner_kernel, half),
        in_specs=[VMEM] * (4 + len(given)),
        out_specs=VMEM if half else [VMEM] * 2,
        out_shape=sums if half else [sums, jax.ShapeDtypeStruct((8, HALF), BF16)],
        scratch_shapes=[pltpu.VMEM((GP, VOX), F32)] * 2,
        compiler_params=params(24),
        cost_estimate=cost(7),
        name="posterior_half",
    )(unit, marks, cbt, codebook, *given)


def border_kernel(last0, last1, bands, following, marks, cbt, codebook, given, out, xh, ue, acc, e0, e1):
    joined = jnp.where(position()[0] < NZ - 1, 1.0, 0.0)
    blocks = NR * PIECE
    for half, last in enumerate((last0, last1)):
        xh[: 4 * STEP] = last[...]

        def store(row, p, t, block):
            start = (4 + row) * STEP + p * CH
            xh[start : start + CH, t * 128 : (t + 1) * 128] = block

        transposed_rows(lambda r, i: following[half * blocks + r * PIECE + i], range(4), store)
        y = jnp.dot(xh[STEP : 7 * STEP], bands[half], preferred_element_type=F32)

        def raw(row, p):
            return xh[row * STEP + p * CH : row * STEP + (p + 1) * CH, :HALF].astype(F32)

        def cols(row, p, twice):
            start = (row - 1) * STEP + p * CH
            return y[start : start + CH, twice * HALF : (twice + 1) * HALF]

        def up(get, row, p):
            return get(row - 1, p) * joined if row == 4 else get(row - 1, p)

        def down(get, row, p):
            return get(row + 1, p) * joined if row == 3 else get(row + 1, p)

        a, b = {}, {}
        for row in range(1, 7):
            for p in range(ZP):
                cx = cols(row, p, 0)
                a[row, p] = vertical(up(raw, row, p), raw(row, p), down(raw, row, p)) - raw(row, 1 - p) - cx
                b[row, p] = a[row, p] - cx

        def get_b(row, p):
            return b[row, p]

        for row in range(2, 6):
            for p in range(ZP):
                mb = vertical(up(get_b, row, p), b[row, p], down(get_b, row, p)) - b[row, 1 - p]
                at = ((row % 2) * ZP + p) * HALF
                ue[half * 2 + row // 2 - 1, :, at : at + HALF] = normalise(
                    a[row, p] + SHARPEN * (mb + cols(row, p, 1))
                )

    acc[...] = given[...]
    tops = [following[2 * blocks + h].astype(F32).astype(jnp.int32) for h in range(2)]

    def mark(k):
        own = [label_row(marks, h, ROWS - 2) for h in range(2)]
        next_ = [
            jnp.concatenate([tops[h][i : i + 1] for i in range(4)], axis=1) for h in range(2)
        ]
        return jnp.where(k < 2, jnp.where(k == 0, own[0], next_[0]), jnp.where(k == 2, own[1], next_[1]))

    posteriors(no_maximum_needed(codebook), 4, lambda k: ue[k], mark, cbt, acc, e0, e1)

    goes = marks[ZP * ROWS : ZP * ROWS + 1]
    select = jnp.where(lax.broadcasted_iota(jnp.int32, (TILES * CAP, CELLS), 0) == goes, SCALE, 0.0).astype(BF16)
    sums = jnp.concatenate([acc[...], jnp.zeros((128 * (FULL + 1) - GP, CELLS), F32)], axis=0)
    high = sums.astype(BF16)
    low = (sums - high.astype(F32)).astype(BF16)
    packed = lax.dot_general(select, high, NT, preferred_element_type=F32)
    packed = packed + lax.dot_general(select, low, NT, preferred_element_type=F32)
    lane = lax.broadcasted_iota(jnp.int32, (CAP // 2, 128), 1)
    for o in range(TILES):
        rows = packed[o * CAP : (o + 1) * CAP]
        for t in range(FULL):
            out[o, t * CAP : (t + 1) * CAP] = rows[:, t * 128 : (t + 1) * 128]
        rest = rows[:, FULL * 128 :]
        out[o, FULL * CAP :] = jnp.where(lane < 64, rest[: CAP // 2], pltpu.roll(rest[CAP // 2 :], 64, 1))


def border(last0, last1, bands, following, marks, cbt, codebook, given):
    return pl.pallas_call(
        border_kernel,
        in_specs=[VMEM] * 8,
        out_specs=VMEM,
        out_shape=jax.ShapeDtypeStruct((TILES, OUT_ROWS, 128), F32),
        scratch_shapes=[
            pltpu.VMEM((8 * STEP, WIDE), BF16),
            pltpu.VMEM((4, CH, VOX), BF16),
            pltpu.VMEM((GP, CELLS), F32),
            pltpu.VMEM((GP, VOX), F32),
            pltpu.VMEM((GP, VOX), F32),
        ],
        compiler_params=params(24),
        cost_estimate=cost(4),
        name="border_rows",
    )(last0, last1, bands, following, marks, cbt, codebook, given)


def unpack_kernel(parts, out):
    for x in range(NXD):
        for r in range(NR):
            src, dst = x * NR + r, NXD * r + x
            for t in range(FULL):
                out[0, dst, :, t * 128 : (t + 1) * 128] = parts[src, t * CAP : (t + 1) * CAP] * (1.0 / SCALE)
            rest = parts[src, FULL * CAP :] * (1.0 / SCALE)
            out[0, dst, : CAP // 2, FULL * 128 :] = rest[:, :REST]
            out[0, dst, CAP // 2 :, FULL * 128 :] = pltpu.roll(rest, 64, 1)[:, :REST]


def unpack(parts):
    return pl.pallas_call(
        unpack_kernel,
        in_specs=[VMEM],
        out_specs=VMEM,
        out_shape=jax.ShapeDtypeStruct((1, TILES, CAP, GENES), F32),
        compiler_params=params(16),
        name="unpack_cells",
    )(parts)


def local(images, labels, counts, owners, codebook):
    swap = [
        (z * NXD * NR + x * NR + r, r * NXD * NR + x * NR + z)
        for z in range(NZ)
        for x in range(NXD)
        for r in range(NR)
    ]
    plane = functools.partial(lax.all_to_all, axis_name=("x", "r"), split_axis=0, concat_axis=0, tiled=True)
    g0 = plane(pack(images, 0))
    g1 = plane(pack(images, 1))
    marks, cbt, bands = prepare(labels, owners.reshape(1, CELLS), counts, codebook)
    marks = lax.ppermute(marks, ("z", "x", "r"), swap)
    unit0, last0 = stencil(g0, bands, 0)
    acc, tops = inner(unit0, marks, cbt, codebook, 0)
    g1, acc, tops = lax.optimization_barrier((g1, acc, tops))
    upper = [g[:NR, :, :4].reshape(NR * PIECE, 4, 128) for g in (g0, g1)]
    upper = jnp.concatenate([*upper, tops.reshape(2, 4, HALF)], axis=0)
    following = lax.ppermute(upper, "z", [((i + 1) % NZ, i) for i in range(NZ)])
    unit1, last1 = stencil(g1, bands, 1)
    acc = inner(unit1, marks, cbt, codebook, 1, acc)
    packed = border(last0, last1, bands, following, marks, cbt, codebook, acc)
    packed = packed.astype(jnp.float16).reshape(NZ, NXD, OUT_ROWS, 128)
    parts = lax.all_to_all(packed, "z", split_axis=0, concat_axis=0, tiled=True)
    summed = jnp.sum(parts.astype(F32), axis=0).astype(jnp.float16)[:, None]
    spread = jnp.broadcast_to(summed, (NXD, NR, OUT_ROWS, 128)).reshape(NXD * NR, OUT_ROWS, 128)
    return unpack(plane(spread).astype(F32))


def solution(mesh):
    grid = Mesh(mesh.devices.reshape(NZ, NXD, NR), ("z", "x", "r"))
    in_specs = (P("r", None, ("z", "x"), None), P(None, "r", ("z", "x")), P(), P(("z", "x"), None), P())
    out_specs = P(("z", "x"), None, None, None)
    return jax.shard_map(local, mesh=grid, in_specs=in_specs, out_specs=out_specs, check_vma=False)
```

```python
import functools

import jax
import jax.numpy as jnp
from jax import lax
from jax.experimental import pallas as pl
from jax.experimental.pallas import tpu as pltpu
from jax.sharding import Mesh, PartitionSpec as P

SOFTMAX_HEAT = 0.6
SHARPEN = 0.15
NOISE_LEVEL = 1.0
LOG2E = 1.4426950408889634

CH, GENES, ZP, PT, CELLS, TILES, CAP = 48, 550, 2, 256, 256, 32, 16
NZ, NXD, NR = 8, 4, 8
GP = 552
COLOUR = CH // NR
PAIRS = COLOUR * ZP
HALF = PT // 2
PIECE = PAIRS + 1
ROWS = 32
STEP = ZP * CH
WIDE = HALF + 128
VOX = 2 * ZP * HALF
MARKS = ZP * ROWS + 8
FULL = GENES // 128
REST = GENES - 128 * FULL
OUT_ROWS = FULL * CAP + CAP // 2
SCALE = 0.25
SAFE = 100.0
F32, BF16 = jnp.float32, jnp.bfloat16
NT = (((1,), (1,)), ((), ()))
VMEM = pl.BlockSpec(memory_space=pltpu.VMEM)
SMEM = pl.BlockSpec(memory_space=pltpu.SMEM)
MIB = 1024 * 1024


def position():
    return lax.axis_index("z"), lax.axis_index("x"), lax.axis_index("r")


def params(mib):
    return pltpu.CompilerParams(vmem_limit_bytes=mib * MIB)


def cost(us):
    return pl.CostEstimate(flops=int(us * 1e9), bytes_accessed=int(us * 3e6), transcendentals=0)


def pack_kernel(img, out, buf, sems):
    lane = lax.broadcasted_iota(jnp.int32, (8, 128), 1)
    windows = [(lane // 4) == i for i in range(PAIRS)]
    width = NXD * PT

    def fetch(r):
        start = pl.multiple_of(r * width, width)
        return pltpu.make_async_copy(img.at[:, :, :, pl.ds(start, width)], buf.at[r], sems.at[r])

    for r in range(NR):
        fetch(r).start()
    fetch(0).wait()

    def column(r, _):
        after, before = jnp.minimum(r + 1, NR - 1), jnp.maximum(r - 1, 0)

        @pl.when(r < NR - 1)
        def _():
            fetch(after).wait()

        has_after, has_before = (r < NR - 1).astype(F32), (r > 0).astype(F32)
        for x in range(NXD):
            for half in range(2):
                at = PT * x + HALF * half
                border = jnp.zeros((8, 128), F32)
                for i in range(PAIRS):
                    c, p = i // ZP, i % ZP
                    out[x * NR + r, half * PIECE + i] = buf[r, c, p, :, at : at + HALF]
                    if at + HALF < width:
                        right = buf[r, c, p, :, at + HALF : at + 2 * HALF].astype(F32)
                    else:
                        right = buf[after, c, p, :, :128].astype(F32) * has_after
                    if at > 0:
                        left = buf[r, c, p, :, at - 128 : at].astype(F32)
                    else:
                        left = buf[before, c, p, :, width - 128 :].astype(F32) * has_before
                    both = pltpu.roll(jnp.where(lane < 64, right, left), 4 * i + 2, 1)
                    border = jnp.where(windows[i], both, border)
                out[x * NR + r, half * PIECE + PAIRS] = border.astype(BF16)
        return 0

    lax.fori_loop(0, NR, column, 0)


def pack(images):
    return pl.pallas_call(
        pack_kernel,
        in_specs=[pl.BlockSpec(memory_space=pltpu.HBM)],
        out_specs=VMEM,
        out_shape=jax.ShapeDtypeStruct((NXD * NR, 2 * PIECE, 8, 128), BF16),
        scratch_shapes=[pltpu.VMEM((NR, COLOUR, ZP, 8, NXD * PT), BF16), pltpu.SemaphoreType.DMA((NR,))],
        compiler_params=params(16),
        cost_estimate=cost(2),
        name="pack_pieces",
    )(pltpu.with_memory_space_constraint(images, pltpu.HBM))


def prepare_kernel(labels, owners, counts, codebook, marks, cbt, bands):
    z, x, r = position()
    owner = owners[...]
    own = lax.broadcasted_iota(jnp.int32, (TILES, CELLS), 0) == owner
    own_f = jnp.where(own, 1.0, 0.0)
    earlier = lax.broadcasted_iota(jnp.int32, (CELLS, CELLS), 0) < lax.broadcasted_iota(jnp.int32, (CELLS, CELLS), 1)
    earlier = jnp.where(earlier, 1.0, 0.0).astype(BF16)
    ahead = jnp.dot(own_f.astype(BF16), earlier, preferred_element_type=F32)
    place = jnp.sum(own_f * ahead, axis=0, keepdims=True).astype(jnp.int32)
    cell = lax.broadcasted_iota(jnp.int32, (1, CELLS), 1)
    goes = jnp.where(cell < counts[NXD * z + x], owner * CAP + place, -1)
    for p in range(ZP):
        marks[p * ROWS : (p + 1) * ROWS] = labels[p]
    marks[ZP * ROWS :] = jnp.broadcast_to(goes, (8, CELLS))

    out_row = lax.broadcasted_iota(jnp.int32, (CH, CH), 0)
    in_row = lax.broadcasted_iota(jnp.int32, (CH, CH), 1)
    order = jnp.where(in_row == (out_row % NR) * COLOUR + out_row // NR, 1.0, 0.0).astype(BF16)
    wide = jnp.dot(order, codebook[...], preferred_element_type=F32) * (SOFTMAX_HEAT * LOG2E)
    flat = jnp.concatenate([wide, jnp.zeros((CH, GP - GENES), F32)], axis=1).T
    hi = flat.astype(BF16)
    mid = (flat - hi.astype(F32)).astype(BF16)
    lo = (flat - hi.astype(F32) - mid.astype(F32)).astype(BF16)
    gene = lax.broadcasted_iota(jnp.int32, (GP, 16), 0)
    which = lax.broadcasted_iota(jnp.int32, (GP, 16), 1)
    shut = jnp.where((gene >= GENES) & (which == 0), -3.0e38, 0.0).astype(BF16)
    cbt[...] = jnp.concatenate([hi, mid, lo, shut], axis=1)

    tile = NXD * r + x
    source = lax.broadcasted_iota(jnp.int32, (WIDE, HALF), 0)
    target = lax.broadcasted_iota(jnp.int32, (WIDE, HALF), 1)
    e = source - HALF
    side = e % 4
    beyond = jnp.where(side < 2, side - 2, HALF - 2 + side)
    at = jnp.where(source < HALF, source, jnp.where(e < 4 * PAIRS, beyond, 4 * WIDE))
    gap = jnp.abs(at - target)
    once = jnp.where(gap == 1, 1.0, 0.0).astype(BF16)
    for half in range(2):
        outer = (tile == TILES - 1) if half else (tile == 0)
        edge = jnp.where(at == (HALF - 1 if half else 0), jnp.where(outer, 1.0, 0.0), 0.0)
        bands[half, :, :HALF] = once
        bands[half, :, HALF:] = jnp.where(gap == 2, 1.0, jnp.where(gap == 0, 2.0 - edge, 0.0)).astype(BF16)


def prepare(labels, owners, counts, codebook):
    return pl.pallas_call(
        prepare_kernel,
        in_specs=[VMEM, VMEM, SMEM, VMEM],
        out_specs=[VMEM] * 3,
        out_shape=[
            jax.ShapeDtypeStruct((MARKS, CELLS), jnp.int32),
            jax.ShapeDtypeStruct((GP, 3 * CH + 16), BF16),
            jax.ShapeDtypeStruct((2, WIDE, 2 * HALF), BF16),
        ],
        compiler_params=params(16),
        cost_estimate=cost(2),
        name="prepare",
    )(labels, owners, counts, codebook)


def transposed_rows(src, rows, store):
    lane = lax.broadcasted_iota(jnp.int32, (CH, 128), 1)
    colour = lax.broadcasted_iota(jnp.int32, (CH, 128), 0) // NR

    def swapped(i):
        return jnp.swapaxes(jnp.stack([src(r, i) for r in range(NR)]).astype(F32), 0, 1)

    edge = swapped(PAIRS)
    for p in range(ZP):
        parts = [swapped(ZP * c + p) for c in range(COLOUR)]
        mask = (lane // 4) == colour * ZP + p
        for row in rows:
            store(row, p, 0, jnp.concatenate([part[row] for part in parts], axis=0).astype(BF16))
            border = jnp.concatenate([edge[row]] * COLOUR, axis=0)
            store(row, p, 1, jnp.where(mask, border, 0.0).astype(BF16))


def normalise(value):
    mean = jnp.sum(value * value, axis=0, keepdims=True) * (1.0 / CH)
    return (value * lax.rsqrt(mean + 49.0 * NOISE_LEVEL)).astype(BF16)


def vertical(first, second, third):
    return 6.0 * second - (first + third)


def stencil_steps(half, g, bands, unit, last, xt, y, a_s, b_s):
    def regroup(k):
        base = k * 8 * STEP

        def store(row, p, t, block):
            start = pl.multiple_of(base + (row * ZP + p) * CH, 16)
            xt[pl.ds(start, CH), t * 128 : (t + 1) * 128] = block

        transposed_rows(lambda r, i: g[k * NR + r, half * PIECE + i], range(8), store)
        at = pl.ds(pl.multiple_of(base, 16), 8 * STEP)
        y[at, :] = jnp.dot(xt[at, :], bands[half], preferred_element_type=F32)

    def keep():
        last[half] = xt[(ROWS - 4) * STEP :]

    def raw(row, p):
        return xt[pl.ds(pl.multiple_of(row * STEP + p * CH, 16), CH), :HALF].astype(F32)

    def cols(row, p, twice):
        return y[pl.ds(pl.multiple_of(row * STEP + p * CH, 16), CH), twice * HALF : (twice + 1) * HALF]

    def first(row):
        here = [raw(row, p) for p in range(ZP)]
        for p in range(ZP):
            cx = cols(row, p, 0)
            a = vertical(raw(row - 1, p), here[p], raw(row + 1, p)) - here[1 - p] - cx
            a_s[row, p] = a
            b_s[row, p] = a - cx

    def second(k):
        for odd in range(2):
            row = 2 * k + odd
            mid = [b_s[row, p] for p in range(ZP)]
            for p in range(ZP):
                mb = vertical(b_s[row - 1, p], mid[p], b_s[row + 1, p]) - mid[1 - p]
                at = (odd * ZP + p) * HALF
                unit[k, :, at : at + HALF] = normalise(a_s[row, p] + SHARPEN * (mb + cols(row, p, 1)))

    return regroup, keep, first, second


def loop(low, high, step):
    def body(k, _):
        step(k)
        return 0

    lax.fori_loop(low, high, body, 0)


def no_maximum_needed(codebook):
    wide = codebook[...].astype(F32)
    longest = jnp.max(jnp.sum(wide * wide, axis=0, keepdims=True))
    return longest * (CH * (1.01 * SOFTMAX_HEAT * LOG2E) ** 2) <= SAFE * SAFE


def posterior_steps(cbt, acc):
    slots = lax.broadcasted_iota(jnp.int32, (CELLS, VOX), 0).astype(F32).astype(BF16)

    def logits_of(u):
        stacked = jnp.concatenate([u, u, u, jnp.ones((16, VOX), BF16)], axis=0)
        return jnp.dot(cbt[...], stacked, preferred_element_type=F32)

    def add(post, label):
        onehot = jnp.where(slots == label.astype(F32).astype(BF16), jnp.ones((), BF16), jnp.zeros((), BF16))
        acc[...] += lax.dot_general(post, onehot, NT, preferred_element_type=F32)

    def begin(u, e_s):
        e = jnp.exp2(logits_of(u))
        e_s[...] = e
        return 1.0 / jnp.sum(e, axis=0, keepdims=True)

    def finish(inverse, label, e_s):
        add((e_s[...] * inverse).astype(BF16), label)

    def careful(u, label):
        logits = logits_of(u)
        e = jnp.exp2(logits - jnp.max(logits, axis=0, keepdims=True))
        add((e * (1.0 / jnp.sum(e, axis=0, keepdims=True))).astype(BF16), label)

    return begin, finish, careful


def label_row(marks, half, row):
    parts = [marks[pl.ds(p * ROWS + row + odd, 1), :] for odd in range(2) for p in range(ZP)]
    return jnp.concatenate([part[:, half * HALF : (half + 1) * HALF] for part in parts], axis=1)


def decode_kernel(g, bands, marks, cbt, codebook, acc, last, xt, y, a_s, b_s, unit0, unit1, e0, e1):
    units = (unit0, unit1)
    acc[...] = jnp.zeros_like(acc)
    begin, finish, careful = posterior_steps(cbt, acc)

    def label(half, k):
        return label_row(marks, half, 2 * k)

    regroup, keep, first, second = stencil_steps(0, g, bands, unit0, last, xt, y, a_s, b_s)
    loop(0, ROWS // 8, regroup)
    keep()
    loop(1, ROWS - 1, first)
    loop(1, ROWS // 2 - 1, second)
    regroup, keep, first, second = stencil_steps(1, g, bands, unit1, last, xt, y, a_s, b_s)
    fine = no_maximum_needed(codebook)

    @pl.when(fine)
    def _():
        def pair(half, k, inv, following):
            unit = units[half]
            nxt = begin(unit[k + 1], e1)
            finish(inv, label(half, k), e0)
            inv = begin(following, e0)
            finish(nxt, label(half, k + 1), e1)
            return inv

        def with_regroup(i, inv):
            regroup(i)
            return pair(0, 2 * i + 1, inv, unit0[2 * i + 3])

        def with_rows(i, inv):
            for j in range(10):
                first(10 * i + j + 1)
            for j in range(5):
                second(5 * i + j)
            return pair(0, 2 * i + 9, inv, unit0[2 * i + 11] if not isinstance(i, int) else unit1[1])

        inv = lax.fori_loop(0, ROWS // 8, with_regroup, begin(unit0[1], e0))
        keep()
        inv = lax.fori_loop(0, 2, with_rows, inv)
        inv = with_rows(2, inv)
        inv = lax.fori_loop(0, 6, lambda i, inv: pair(1, 2 * i + 1, inv, unit1[2 * i + 3]), inv)
        nxt = begin(unit1[14], e1)
        finish(inv, label(1, 13), e0)
        finish(nxt, label(1, 14), e1)

    @pl.when(jnp.logical_not(fine))
    def _():
        loop(0, ROWS // 8, regroup)
        keep()
        loop(1, ROWS - 1, first)
        loop(1, ROWS // 2 - 1, second)
        for half in range(2):
            loop(1, ROWS // 2 - 1, lambda k: careful(units[half][k], label(half, k)))


def decode(g, bands, marks, cbt, codebook):
    return pl.pallas_call(
        decode_kernel,
        in_specs=[VMEM] * 5,
        out_specs=[VMEM] * 2,
        out_shape=[
            jax.ShapeDtypeStruct((GP, CELLS), F32),
            jax.ShapeDtypeStruct((2, 4 * STEP, WIDE), BF16),
        ],
        scratch_shapes=[
            pltpu.VMEM((ROWS * STEP, WIDE), BF16),
            pltpu.VMEM((ROWS * STEP, 2 * HALF), F32),
            pltpu.VMEM((ROWS, ZP, CH, HALF), F32),
            pltpu.VMEM((ROWS, ZP, CH, HALF), F32),
            pltpu.VMEM((ROWS // 2, CH, VOX), BF16),
            pltpu.VMEM((ROWS // 2, CH, VOX), BF16),
            pltpu.VMEM((GP, VOX), F32),
            pltpu.VMEM((GP, VOX), F32),
        ],
        compiler_params=params(36),
        cost_estimate=cost(15),
        name="decode_band",
    )(g, bands, marks, cbt, codebook)


def border_kernel(last, bands, following, marks, cbt, codebook, given, out, xh, ue, acc, e0, e1):
    joined = jnp.where(position()[0] < NZ - 1, 1.0, 0.0)
    blocks = 2 * PIECE
    for half in range(2):
        xh[: 4 * STEP] = last[half]

        def store(row, p, t, block):
            start = (4 + row) * STEP + p * CH
            xh[start : start + CH, t * 128 : (t + 1) * 128] = block

        transposed_rows(lambda r, i: following[r * blocks + half * PIECE + i], range(4), store)
        y = jnp.dot(xh[STEP : 7 * STEP], bands[half], preferred_element_type=F32)

        def raw(row, p):
            return xh[row * STEP + p * CH : row * STEP + (p + 1) * CH, :HALF].astype(F32)

        def cols(row, p, twice):
            start = (row - 1) * STEP + p * CH
            return y[start : start + CH, twice * HALF : (twice + 1) * HALF]

        def up(get, row, p):
            return get(row - 1, p) * joined if row == 4 else get(row - 1, p)

        def down(get, row, p):
            return get(row + 1, p) * joined if row == 3 else get(row + 1, p)

        a, b = {}, {}
        for row in range(1, 7):
            for p in range(ZP):
                cx = cols(row, p, 0)
                a[row, p] = vertical(up(raw, row, p), raw(row, p), down(raw, row, p)) - raw(row, 1 - p) - cx
                b[row, p] = a[row, p] - cx

        def get_b(row, p):
            return b[row, p]

        for row in range(2, 6):
            for p in range(ZP):
                mb = vertical(up(get_b, row, p), b[row, p], down(get_b, row, p)) - b[row, 1 - p]
                at = ((row % 2) * ZP + p) * HALF
                ue[half * 2 + row // 2 - 1, :, at : at + HALF] = normalise(
                    a[row, p] + SHARPEN * (mb + cols(row, p, 1))
                )

    acc[...] = given[...]
    tops = [following[NR * blocks + h].astype(F32).astype(jnp.int32) for h in range(2)]

    def mark(k):
        own = [label_row(marks, h, ROWS - 2) for h in range(2)]
        next_ = [
            jnp.concatenate([tops[h][i : i + 1] for i in range(4)], axis=1) for h in range(2)
        ]
        return jnp.where(k < 2, jnp.where(k == 0, own[0], next_[0]), jnp.where(k == 2, own[1], next_[1]))

    begin, finish, careful = posterior_steps(cbt, acc)
    fine = no_maximum_needed(codebook)

    @pl.when(fine)
    def _():
        inv = begin(ue[0], e0)
        nxt = begin(ue[1], e1)
        finish(inv, mark(0), e0)
        inv = begin(ue[2], e0)
        finish(nxt, mark(1), e1)
        nxt = begin(ue[3], e1)
        finish(inv, mark(2), e0)
        finish(nxt, mark(3), e1)

    @pl.when(jnp.logical_not(fine))
    def _():
        loop(0, 4, lambda k: careful(ue[k], mark(k)))

    goes = marks[ZP * ROWS : ZP * ROWS + 1]
    select = jnp.where(lax.broadcasted_iota(jnp.int32, (TILES * CAP, CELLS), 0) == goes, SCALE, 0.0).astype(BF16)
    sums = jnp.concatenate([acc[...], jnp.zeros((128 * (FULL + 1) - GP, CELLS), F32)], axis=0)
    high = sums.astype(BF16)
    low = (sums - high.astype(F32)).astype(BF16)
    packed = lax.dot_general(select, high, NT, preferred_element_type=F32)
    packed = packed + lax.dot_general(select, low, NT, preferred_element_type=F32)
    lane = lax.broadcasted_iota(jnp.int32, (CAP // 2, 128), 1)
    for o in range(TILES):
        rows = packed[o * CAP : (o + 1) * CAP]
        for t in range(FULL):
            out[o, t * CAP : (t + 1) * CAP] = rows[:, t * 128 : (t + 1) * 128]
        rest = rows[:, FULL * 128 :]
        out[o, FULL * CAP :] = jnp.where(lane < 64, rest[: CAP // 2], pltpu.roll(rest[CAP // 2 :], 64, 1))


def border(last, bands, following, marks, cbt, codebook, given):
    return pl.pallas_call(
        border_kernel,
        in_specs=[VMEM] * 7,
        out_specs=VMEM,
        out_shape=jax.ShapeDtypeStruct((TILES, OUT_ROWS, 128), F32),
        scratch_shapes=[
            pltpu.VMEM((8 * STEP, WIDE), BF16),
            pltpu.VMEM((4, CH, VOX), BF16),
            pltpu.VMEM((GP, CELLS), F32),
            pltpu.VMEM((GP, VOX), F32),
            pltpu.VMEM((GP, VOX), F32),
        ],
        compiler_params=params(24),
        cost_estimate=cost(4),
        name="border_rows",
    )(last, bands, following, marks, cbt, codebook, given)


def unpack_kernel(parts, out):
    for x in range(NXD):
        for r in range(NR):
            src, dst = x * NR + r, NXD * r + x
            for t in range(FULL):
                out[0, dst, :, t * 128 : (t + 1) * 128] = parts[src, t * CAP : (t + 1) * CAP] * (1.0 / SCALE)
            rest = parts[src, FULL * CAP :] * (1.0 / SCALE)
            out[0, dst, : CAP // 2, FULL * 128 :] = rest[:, :REST]
            out[0, dst, CAP // 2 :, FULL * 128 :] = pltpu.roll(rest, 64, 1)[:, :REST]


def unpack(parts):
    return pl.pallas_call(
        unpack_kernel,
        in_specs=[VMEM],
        out_specs=VMEM,
        out_shape=jax.ShapeDtypeStruct((1, TILES, CAP, GENES), F32),
        compiler_params=params(16),
        name="unpack_cells",
    )(parts)


def local(images, labels, counts, owners, codebook):
    swap = [
        (z * NXD * NR + x * NR + r, r * NXD * NR + x * NR + z)
        for z in range(NZ)
        for x in range(NXD)
        for r in range(NR)
    ]
    plane = functools.partial(lax.all_to_all, axis_name=("x", "r"), split_axis=0, concat_axis=0, tiled=True)
    g = plane(pack(images))
    marks, cbt, bands = prepare(labels, owners.reshape(1, CELLS), counts, codebook)
    marks = lax.ppermute(marks, ("z", "x", "r"), swap)
    tops = marks[: ZP * ROWS].reshape(ZP, ROWS, 2, HALF)[:, :2].transpose(2, 1, 0, 3).reshape(2, 4, HALF)
    upper = jnp.concatenate([g[:NR, :, :4].reshape(NR * 2 * PIECE, 4, 128), tops.astype(BF16)], axis=0)
    following = lax.ppermute(upper, "z", [((i + 1) % NZ, i) for i in range(NZ)])
    acc, last = decode(g, bands, marks, cbt, codebook)
    packed = border(last, bands, following, marks, cbt, codebook, acc)
    packed = packed.astype(jnp.float16).reshape(NZ, NXD, OUT_ROWS, 128)
    parts = lax.all_to_all(packed, "z", split_axis=0, concat_axis=0, tiled=True)
    summed = jnp.sum(parts.astype(F32), axis=0).astype(jnp.float16)[:, None]
    spread = jnp.broadcast_to(summed, (NXD, NR, OUT_ROWS, 128)).reshape(NXD * NR, OUT_ROWS, 128)
    return unpack(plane(spread).astype(F32))


def solution(mesh):
    grid = Mesh(mesh.devices.reshape(NZ, NXD, NR), ("z", "x", "r"))
    in_specs = (P("r", None, ("z", "x"), None), P(None, "r", ("z", "x")), P(), P(("z", "x"), None), P())
    out_specs = P(("z", "x"), None, None, None)
    return jax.shard_map(local, mesh=grid, in_specs=in_specs, out_specs=out_specs, check_vma=False)
```

```python
import functools

import jax
import jax.numpy as jnp
from jax import lax
from jax.experimental import pallas as pl
from jax.experimental.pallas import tpu as pltpu
from jax.sharding import Mesh, PartitionSpec as P

SOFTMAX_HEAT = 0.6
SHARPEN = 0.15
NOISE_LEVEL = 1.0
LOG2E = 1.4426950408889634

CH, GENES, ZP, PT, CELLS, TILES, CAP = 48, 550, 2, 256, 256, 32, 16
NZ, NXD, NR = 8, 4, 8
GP = 552
COLOUR = CH // NR
PAIRS = COLOUR * ZP
HALF = PT // 2
PIECE = 2 * PAIRS + 1
ROWS = 32
STEP = ZP * CH
WIDE = HALF + 128
VOX = 2 * ZP * HALF
MARKS = ZP * ROWS + 8
FULL = GENES // 128
REST = GENES - 128 * FULL
OUT_ROWS = FULL * CAP + CAP // 2
SCALE = 0.25
SAFE = 100.0
F32, BF16 = jnp.float32, jnp.bfloat16
NT = (((1,), (1,)), ((), ()))
VMEM = pl.BlockSpec(memory_space=pltpu.VMEM)
SMEM = pl.BlockSpec(memory_space=pltpu.SMEM)
MIB = 1024 * 1024


def position():
    return lax.axis_index("z"), lax.axis_index("x"), 2 * lax.axis_index("y") + lax.axis_index("c")


def params(mib):
    return pltpu.CompilerParams(vmem_limit_bytes=mib * MIB)


def cost(us):
    return pl.CostEstimate(flops=int(us * 1e9), bytes_accessed=int(us * 3e6), transcendentals=0)


def pack_kernel(img, out, buf, sems):
    lane = lax.broadcasted_iota(jnp.int32, (8, 128), 1)
    windows = [(lane // 4) == 16 * half + i for half in range(2) for i in range(PAIRS)]
    width = NXD * PT

    def fetch(r):
        start = pl.multiple_of(r * width, width)
        return pltpu.make_async_copy(img.at[:, :, :, pl.ds(start, width)], buf.at[r], sems.at[r])

    for r in range(NR):
        fetch(r).start()
    fetch(0).wait()

    def column(r, _):
        after, before = jnp.minimum(r + 1, NR - 1), jnp.maximum(r - 1, 0)

        @pl.when(r < NR - 1)
        def _():
            fetch(after).wait()

        has_after, has_before = (r < NR - 1).astype(F32), (r > 0).astype(F32)
        for x in range(NXD):
            border = jnp.zeros((8, 128), F32)
            for half in range(2):
                at = PT * x + HALF * half
                for i in range(PAIRS):
                    c, p = i // ZP, i % ZP
                    out[x * NR + r, half * PAIRS + i] = buf[r, c, p, :, at : at + HALF]
                    if at + HALF < width:
                        right = buf[r, c, p, :, at + HALF : at + 2 * HALF].astype(F32)
                    else:
                        right = buf[after, c, p, :, :128].astype(F32) * has_after
                    if at > 0:
                        left = buf[r, c, p, :, at - 128 : at].astype(F32)
                    else:
                        left = buf[before, c, p, :, width - 128 :].astype(F32) * has_before
                    both = pltpu.roll(jnp.where(lane < 64, right, left), 64 * half + 4 * i + 2, 1)
                    border = jnp.where(windows[half * PAIRS + i], both, border)
            out[x * NR + r, 2 * PAIRS] = border.astype(BF16)
        return 0

    lax.fori_loop(0, NR, column, 0)


def pack(images):
    return pl.pallas_call(
        pack_kernel,
        in_specs=[pl.BlockSpec(memory_space=pltpu.HBM)],
        out_specs=VMEM,
        out_shape=jax.ShapeDtypeStruct((NXD * NR, PIECE, 8, 128), BF16),
        scratch_shapes=[pltpu.VMEM((NR, COLOUR, ZP, 8, NXD * PT), BF16), pltpu.SemaphoreType.DMA((NR,))],
        compiler_params=params(16),
        cost_estimate=cost(2),
        name="pack_pieces",
    )(pltpu.with_memory_space_constraint(images, pltpu.HBM))


def prepare_kernel(labels, owners, counts, codebook, marks, cbt, bands):
    z, x, r = position()
    owner = owners[...]
    own = lax.broadcasted_iota(jnp.int32, (TILES, CELLS), 0) == owner
    own_f = jnp.where(own, 1.0, 0.0)
    earlier = lax.broadcasted_iota(jnp.int32, (CELLS, CELLS), 0) < lax.broadcasted_iota(jnp.int32, (CELLS, CELLS), 1)
    earlier = jnp.where(earlier, 1.0, 0.0).astype(BF16)
    ahead = jnp.dot(own_f.astype(BF16), earlier, preferred_element_type=F32)
    place = jnp.sum(own_f * ahead, axis=0, keepdims=True).astype(jnp.int32)
    cell = lax.broadcasted_iota(jnp.int32, (1, CELLS), 1)
    goes = jnp.where(cell < counts[NXD * z + x], owner * CAP + place, -1)
    for p in range(ZP):
        marks[p * ROWS : (p + 1) * ROWS] = labels[p]
    marks[ZP * ROWS :] = jnp.broadcast_to(goes, (8, CELLS))

    out_row = lax.broadcasted_iota(jnp.int32, (CH, CH), 0)
    in_row = lax.broadcasted_iota(jnp.int32, (CH, CH), 1)
    order = jnp.where(in_row == (out_row % NR) * COLOUR + out_row // NR, 1.0, 0.0).astype(BF16)
    wide = jnp.dot(order, codebook[...], preferred_element_type=F32) * (SOFTMAX_HEAT * LOG2E)
    flat = jnp.concatenate([wide, jnp.zeros((CH, GP - GENES), F32)], axis=1).T
    hi = flat.astype(BF16)
    mid = (flat - hi.astype(F32)).astype(BF16)
    lo = (flat - hi.astype(F32) - mid.astype(F32)).astype(BF16)
    gene = lax.broadcasted_iota(jnp.int32, (GP, 16), 0)
    which = lax.broadcasted_iota(jnp.int32, (GP, 16), 1)
    shut = jnp.where((gene >= GENES) & (which == 0), -3.0e38, 0.0).astype(BF16)
    cbt[...] = jnp.concatenate([hi, mid, lo, shut], axis=1)

    tile = NXD * r + x
    source = lax.broadcasted_iota(jnp.int32, (WIDE, HALF), 0)
    target = lax.broadcasted_iota(jnp.int32, (WIDE, HALF), 1)
    e = source - HALF
    side = e % 4
    beyond = jnp.where(side < 2, side - 2, HALF - 2 + side)
    at = jnp.where(source < HALF, source, jnp.where(e % 64 < 4 * PAIRS, beyond, 4 * WIDE))
    gap = jnp.abs(at - target)
    once = jnp.where(gap == 1, 1.0, 0.0).astype(BF16)
    for half in range(2):
        outer = (tile == TILES - 1) if half else (tile == 0)
        edge = jnp.where(at == (HALF - 1 if half else 0), jnp.where(outer, 1.0, 0.0), 0.0)
        bands[half, :, :HALF] = once
        bands[half, :, HALF:] = jnp.where(gap == 2, 1.0, jnp.where(gap == 0, 2.0 - edge, 0.0)).astype(BF16)


def prepare(labels, owners, counts, codebook):
    return pl.pallas_call(
        prepare_kernel,
        in_specs=[VMEM, VMEM, SMEM, VMEM],
        out_specs=[VMEM] * 3,
        out_shape=[
            jax.ShapeDtypeStruct((MARKS, CELLS), jnp.int32),
            jax.ShapeDtypeStruct((GP, 3 * CH + 16), BF16),
            jax.ShapeDtypeStruct((2, WIDE, 2 * HALF), BF16),
        ],
        compiler_params=params(16),
        cost_estimate=cost(2),
        name="prepare",
    )(labels, owners, counts, codebook)


def transposed_rows(half, src, rows, store):
    lane = lax.broadcasted_iota(jnp.int32, (CH, 128), 1)
    colour = lax.broadcasted_iota(jnp.int32, (CH, 128), 0) // NR

    def swapped(i):
        return jnp.swapaxes(jnp.stack([src(r, i) for r in range(NR)]).astype(F32), 0, 1)

    edge = swapped(2 * PAIRS)
    for p in range(ZP):
        parts = [swapped(half * PAIRS + ZP * c + p) for c in range(COLOUR)]
        mask = (lane // 4) == 16 * half + colour * ZP + p
        for row in rows:
            store(row, p, 0, jnp.concatenate([part[row] for part in parts], axis=0).astype(BF16))
            border = jnp.concatenate([edge[row]] * COLOUR, axis=0)
            store(row, p, 1, jnp.where(mask, border, 0.0).astype(BF16))


def normalise(value):
    mean = jnp.sum(value * value, axis=0, keepdims=True) * (1.0 / CH)
    return (value * lax.rsqrt(mean + 49.0 * NOISE_LEVEL)).astype(BF16)


def vertical(first, second, third):
    return 6.0 * second - (first + third)


def rows_at(start, size):
    return pl.ds(start if isinstance(start, int) else pl.multiple_of(start, 16), size)


def stencil_steps(half, g, bands, unit, last, xt, y, a_s, b_s):
    def regroup(k):
        base = k * 8 * STEP

        def store(row, p, t, block):
            xt[rows_at(base + (row * ZP + p) * CH, CH), t * 128 : (t + 1) * 128] = block

        transposed_rows(half, lambda r, i: g[k * NR + r, i], range(8), store)
        at = rows_at(base, 8 * STEP)
        y[at, :] = jnp.dot(xt[at, :], bands[half], preferred_element_type=F32)

    def keep():
        last[half] = xt[(ROWS - 4) * STEP :]

    def raw(row, p):
        return xt[rows_at(row * STEP + p * CH, CH), :HALF].astype(F32)

    def cols(row, p, twice):
        return y[rows_at(row * STEP + p * CH, CH), twice * HALF : (twice + 1) * HALF]

    def first(row):
        here = [raw(row, p) for p in range(ZP)]
        for p in range(ZP):
            cx = cols(row, p, 0)
            a = vertical(raw(row - 1, p), here[p], raw(row + 1, p)) - here[1 - p] - cx
            a_s[row, p] = a
            b_s[row, p] = a - cx

    def second(k):
        for odd in range(2):
            row = 2 * k + odd
            mid = [b_s[row, p] for p in range(ZP)]
            for p in range(ZP):
                mb = vertical(b_s[row - 1, p], mid[p], b_s[row + 1, p]) - mid[1 - p]
                at = (odd * ZP + p) * HALF
                unit[k, :, at : at + HALF] = normalise(a_s[row, p] + SHARPEN * (mb + cols(row, p, 1)))

    return regroup, keep, first, second


def loop(low, high, step):
    def body(k, _):
        step(k)
        return 0

    lax.fori_loop(low, high, body, 0)


def no_maximum_needed(codebook):
    wide = codebook[...].astype(F32)
    longest = jnp.max(jnp.sum(wide * wide, axis=0, keepdims=True))
    return longest * (CH * (1.01 * SOFTMAX_HEAT * LOG2E) ** 2) <= SAFE * SAFE


def posterior_steps(cbt, acc):
    slots = lax.broadcasted_iota(jnp.int32, (CELLS, VOX), 0).astype(F32).astype(BF16)

    def logits_of(u):
        stacked = jnp.concatenate([u, u, u, jnp.ones((16, VOX), BF16)], axis=0)
        return jnp.dot(cbt[...], stacked, preferred_element_type=F32)

    def add(post, label):
        onehot = jnp.where(slots == label.astype(F32).astype(BF16), jnp.ones((), BF16), jnp.zeros((), BF16))
        acc[...] += lax.dot_general(post, onehot, NT, preferred_element_type=F32)

    def begin(u, e_s):
        e = jnp.exp2(logits_of(u))
        e_s[...] = e
        return 1.0 / jnp.sum(e, axis=0, keepdims=True)

    def finish(inverse, label, e_s):
        add((e_s[...] * inverse).astype(BF16), label)

    def careful(u, label):
        logits = logits_of(u)
        e = jnp.exp2(logits - jnp.max(logits, axis=0, keepdims=True))
        add((e * (1.0 / jnp.sum(e, axis=0, keepdims=True))).astype(BF16), label)

    return begin, finish, careful


def label_row(marks, half, row):
    parts = [marks[pl.ds(p * ROWS + row + odd, 1), :] for odd in range(2) for p in range(ZP)]
    return jnp.concatenate([part[:, half * HALF : (half + 1) * HALF] for part in parts], axis=1)


def decode_kernel(g, bands, marks, cbt, codebook, acc, last, xt, y, a_s, b_s, unit0, unit1, e0, e1):
    units, buffers = (unit0, unit1), (e0, e1)
    acc[...] = jnp.zeros_like(acc)
    begin, finish, careful = posterior_steps(cbt, acc)
    halves = [stencil_steps(half, g, bands, units[half], last, xt, y, a_s, b_s) for half in range(2)]
    fine = no_maximum_needed(codebook)

    def label(half, k):
        return label_row(marks, half, 2 * k)

    def block(half, k):
        regroup, keep, first, second = halves[half]
        regroup(k)
        if k == ROWS // 8 - 1:
            keep()
        for row in range(max(8 * k - 1, 1), 8 * k + 7):
            first(row)
        pairs = list(range(max(4 * k - 1, 1), 4 * k + 3))
        for pair in pairs:
            second(pair)
        return [(half, pair) for pair in pairs]

    @pl.when(fine)
    def _():
        blocks = [(half, k) for half in range(2) for k in range(ROWS // 8)]
        ready = block(*blocks[0])
        started = None
        for number in range(len(blocks)):
            coming = block(*blocks[number + 1]) if number + 1 < len(blocks) else []
            for n, (half, pair) in enumerate(ready):
                if started is None:
                    started = (0, begin(units[half][pair], buffers[0]))
                slot, inverse = started
                following = (ready[n + 1 :] + coming)[:1]
                started = None
                for half2, pair2 in following:
                    started = (1 - slot, begin(units[half2][pair2], buffers[1 - slot]))
                finish(inverse, label(half, pair), buffers[slot])
            ready = coming

    @pl.when(jnp.logical_not(fine))
    def _():
        for half, (regroup, keep, first, second) in enumerate(halves):
            loop(0, ROWS // 8, regroup)
            keep()
            loop(1, ROWS - 1, first)
            loop(1, ROWS // 2 - 1, second)
            loop(1, ROWS // 2 - 1, lambda k: careful(units[half][k], label(half, k)))


def decode(g, bands, marks, cbt, codebook):
    return pl.pallas_call(
        decode_kernel,
        in_specs=[VMEM] * 5,
        out_specs=[VMEM] * 2,
        out_shape=[
            jax.ShapeDtypeStruct((GP, CELLS), F32),
            jax.ShapeDtypeStruct((2, 4 * STEP, WIDE), BF16),
        ],
        scratch_shapes=[
            pltpu.VMEM((ROWS * STEP, WIDE), BF16),
            pltpu.VMEM((ROWS * STEP, 2 * HALF), F32),
            pltpu.VMEM((ROWS, ZP, CH, HALF), F32),
            pltpu.VMEM((ROWS, ZP, CH, HALF), F32),
            pltpu.VMEM((ROWS // 2, CH, VOX), BF16),
            pltpu.VMEM((ROWS // 2, CH, VOX), BF16),
            pltpu.VMEM((GP, VOX), F32),
            pltpu.VMEM((GP, VOX), F32),
        ],
        compiler_params=params(36),
        cost_estimate=cost(15),
        name="decode_band",
    )(g, bands, marks, cbt, codebook)


def border_kernel(last, bands, following, marks, cbt, codebook, given, out, xh, ue, acc, e0, e1):
    joined = jnp.where(position()[0] < NZ - 1, 1.0, 0.0)

    def prepare_units():
        for half in range(2):
            xh[: 4 * STEP] = last[half]

            def store(row, p, t, block):
                start = (4 + row) * STEP + p * CH
                xh[start : start + CH, t * 128 : (t + 1) * 128] = block

            transposed_rows(half, lambda r, i: following[r * PIECE + i], range(4), store)
            y = jnp.dot(xh[STEP : 7 * STEP], bands[half], preferred_element_type=F32)

            def raw(row, p):
                return xh[row * STEP + p * CH : row * STEP + (p + 1) * CH, :HALF].astype(F32)

            def cols(row, p, twice):
                start = (row - 1) * STEP + p * CH
                return y[start : start + CH, twice * HALF : (twice + 1) * HALF]

            def up(get, row, p):
                return get(row - 1, p) * joined if row == 4 else get(row - 1, p)

            def down(get, row, p):
                return get(row + 1, p) * joined if row == 3 else get(row + 1, p)

            a, b = {}, {}
            for row in range(1, 7):
                for p in range(ZP):
                    cx = cols(row, p, 0)
                    a[row, p] = vertical(up(raw, row, p), raw(row, p), down(raw, row, p)) - raw(row, 1 - p) - cx
                    b[row, p] = a[row, p] - cx

            def get_b(row, p):
                return b[row, p]

            for row in range(2, 6):
                for p in range(ZP):
                    mb = vertical(up(get_b, row, p), b[row, p], down(get_b, row, p)) - b[row, 1 - p]
                    at = ((row % 2) * ZP + p) * HALF
                    ue[half * 2 + row // 2 - 1, :, at : at + HALF] = normalise(
                        a[row, p] + SHARPEN * (mb + cols(row, p, 1))
                    )

    acc[...] = given[...]
    tops = [following[NR * PIECE + h].astype(F32).astype(jnp.int32) for h in range(2)]

    def mark(k):
        own = [label_row(marks, h, ROWS - 2) for h in range(2)]
        next_ = [
            jnp.concatenate([tops[h][i : i + 1] for i in range(4)], axis=1) for h in range(2)
        ]
        return jnp.where(k < 2, jnp.where(k == 0, own[0], next_[0]), jnp.where(k == 2, own[1], next_[1]))

    begin, finish, careful = posterior_steps(cbt, acc)
    fine = no_maximum_needed(codebook)

    @pl.when(fine)
    def _():
        prepare_units()
        inv = begin(ue[0], e0)
        nxt = begin(ue[1], e1)
        finish(inv, mark(0), e0)
        inv = begin(ue[2], e0)
        finish(nxt, mark(1), e1)
        nxt = begin(ue[3], e1)
        finish(inv, mark(2), e0)
        finish(nxt, mark(3), e1)

    @pl.when(jnp.logical_not(fine))
    def _():
        prepare_units()
        loop(0, 4, lambda k: careful(ue[k], mark(k)))

    goes = marks[ZP * ROWS : ZP * ROWS + 1]
    select = jnp.where(lax.broadcasted_iota(jnp.int32, (TILES * CAP, CELLS), 0) == goes, SCALE, 0.0).astype(BF16)
    sums = jnp.concatenate([acc[...], jnp.zeros((128 * (FULL + 1) - GP, CELLS), F32)], axis=0)
    high = sums.astype(BF16)
    low = (sums - high.astype(F32)).astype(BF16)
    packed = lax.dot_general(select, high, NT, preferred_element_type=F32)
    packed = packed + lax.dot_general(select, low, NT, preferred_element_type=F32)
    lane = lax.broadcasted_iota(jnp.int32, (CAP // 2, 128), 1)
    for o in range(TILES):
        rows = packed[o * CAP : (o + 1) * CAP]
        for t in range(FULL):
            out[o, t * CAP : (t + 1) * CAP] = rows[:, t * 128 : (t + 1) * 128]
        rest = rows[:, FULL * 128 :]
        out[o, FULL * CAP :] = jnp.where(lane < 64, rest[: CAP // 2], pltpu.roll(rest[CAP // 2 :], 64, 1))


def border(last, bands, following, marks, cbt, codebook, given):
    return pl.pallas_call(
        border_kernel,
        in_specs=[VMEM] * 7,
        out_specs=VMEM,
        out_shape=jax.ShapeDtypeStruct((TILES, OUT_ROWS, 128), F32),
        scratch_shapes=[
            pltpu.VMEM((8 * STEP, WIDE), BF16),
            pltpu.VMEM((4, CH, VOX), BF16),
            pltpu.VMEM((GP, CELLS), F32),
            pltpu.VMEM((GP, VOX), F32),
            pltpu.VMEM((GP, VOX), F32),
        ],
        compiler_params=params(24),
        cost_estimate=cost(4),
        name="border_rows",
    )(last, bands, following, marks, cbt, codebook, given)


def unpack_kernel(parts, out):
    for core in range(2):
        for x in range(NXD):
            for y in range(NR // 2):
                src, dst = (core * NXD + x) * (NR // 2) + y, NXD * (2 * y + core) + x
                for t in range(FULL):
                    out[0, dst, :, t * 128 : (t + 1) * 128] = parts[src, t * CAP : (t + 1) * CAP] * (1.0 / SCALE)
                rest = parts[src, FULL * CAP :] * (1.0 / SCALE)
                out[0, dst, : CAP // 2, FULL * 128 :] = rest[:, :REST]
                out[0, dst, CAP // 2 :, FULL * 128 :] = pltpu.roll(rest, 64, 1)[:, :REST]


def unpack(parts):
    return pl.pallas_call(
        unpack_kernel,
        in_specs=[VMEM],
        out_specs=VMEM,
        out_shape=jax.ShapeDtypeStruct((1, TILES, CAP, GENES), F32),
        compiler_params=params(16),
        name="unpack_cells",
    )(parts)


def local(images, labels, counts, owners, codebook):
    swap = [
        (z * NXD * NR + x * NR + r, r * NXD * NR + x * NR + z)
        for z in range(NZ)
        for x in range(NXD)
        for r in range(NR)
    ]
    exchange = functools.partial(lax.all_to_all, split_axis=0, concat_axis=0, tiled=True)
    g = exchange(pack(images), ("x", "y", "c"))
    marks, cbt, bands = prepare(labels, owners.reshape(1, CELLS), counts, codebook)
    marks = lax.ppermute(marks, ("z", "x", "y", "c"), swap)
    tops = marks[: ZP * ROWS].reshape(ZP, ROWS, 2, HALF)[:, :2].transpose(2, 1, 0, 3).reshape(2, 4, HALF)
    upper = jnp.concatenate([g[:NR, :, :4].reshape(NR * PIECE, 4, 128), tops.astype(BF16)], axis=0)
    following = lax.ppermute(upper, "z", [((i + 1) % NZ, i) for i in range(NZ)])
    acc, last = decode(g, bands, marks, cbt, codebook)
    packed = border(last, bands, following, marks, cbt, codebook, acc)
    packed = packed.astype(jnp.float16).reshape(NZ, NXD, OUT_ROWS, 128)
    parts = exchange(packed, "z")
    summed = jnp.sum(parts.astype(F32), axis=0).astype(jnp.float16)[:, None]
    spread = jnp.broadcast_to(summed, (NXD, NR // 2, OUT_ROWS, 128)).reshape(NXD * NR // 2, OUT_ROWS, 128)
    received = lax.all_gather(exchange(spread, ("x", "y")), "c", tiled=True)
    return unpack(received.astype(F32))


def solution(mesh):
    grid = Mesh(mesh.devices.reshape(NZ, NXD, NR // 2, 2), ("z", "x", "y", "c"))
    rounds = ("y", "c")
    in_specs = (P(rounds, None, ("z", "x"), None), P(None, rounds, ("z", "x")), P(), P(("z", "x"), None), P())
    out_specs = P(("z", "x"), None, None, None)
    return jax.shard_map(local, mesh=grid, in_specs=in_specs, out_specs=out_specs, check_vma=False)
```

```python
import functools

import jax
import jax.numpy as jnp
from jax import lax
from jax.experimental import pallas as pl
from jax.experimental.pallas import tpu as pltpu
from jax.sharding import Mesh, PartitionSpec as P

SOFTMAX_HEAT = 0.6
SHARPEN = 0.15
NOISE_LEVEL = 1.0
LOG2E = 1.4426950408889634

CH, GENES, ZP, PT, CELLS, TILES, CAP = 48, 550, 2, 256, 256, 32, 16
NZ, NXD, NR = 8, 4, 8
GP = 552
COLOUR = CH // NR
PAIRS = COLOUR * ZP
HALF = PT // 2
PIECE = 2 * PAIRS + 1
ROWS = 32
STEP = ZP * CH
WIDE = HALF + 128
VOX = 2 * ZP * HALF
MARKS = ZP * ROWS + 8
FULL = GENES // 128
REST = GENES - 128 * FULL
OUT_ROWS = FULL * CAP + CAP // 2
SCALE = 0.25
SAFE = 100.0
F32, BF16 = jnp.float32, jnp.bfloat16
NT = (((1,), (1,)), ((), ()))
VMEM = pl.BlockSpec(memory_space=pltpu.VMEM)
SMEM = pl.BlockSpec(memory_space=pltpu.SMEM)
MIB = 1024 * 1024


def position():
    return lax.axis_index("z"), lax.axis_index("x"), 2 * lax.axis_index("y") + lax.axis_index("c")


def params(mib):
    return pltpu.CompilerParams(vmem_limit_bytes=mib * MIB)


def cost(us):
    return pl.CostEstimate(flops=int(us * 1e9), bytes_accessed=int(us * 3e6), transcendentals=0)


def pack_kernel(img, out, buf, sems):
    lane = lax.broadcasted_iota(jnp.int32, (8, 128), 1)
    windows = [(lane // 4) == 16 * half + i for half in range(2) for i in range(PAIRS)]
    width = NXD * PT

    def fetch(r):
        start = pl.multiple_of(r * width, width)
        return pltpu.make_async_copy(img.at[:, :, :, pl.ds(start, width)], buf.at[r], sems.at[r])

    for r in range(NR):
        fetch(r).start()
    fetch(0).wait()

    def column(r, _):
        after, before = jnp.minimum(r + 1, NR - 1), jnp.maximum(r - 1, 0)

        @pl.when(r < NR - 1)
        def _():
            fetch(after).wait()

        has_after, has_before = (r < NR - 1).astype(F32), (r > 0).astype(F32)
        for x in range(NXD):
            border = jnp.zeros((8, 128), F32)
            for half in range(2):
                at = PT * x + HALF * half
                for i in range(PAIRS):
                    c, p = i // ZP, i % ZP
                    out[x * NR + r, half * PAIRS + i] = buf[r, c, p, :, at : at + HALF]
                    if at + HALF < width:
                        right = buf[r, c, p, :, at + HALF : at + 2 * HALF].astype(F32)
                    else:
                        right = buf[after, c, p, :, :128].astype(F32) * has_after
                    if at > 0:
                        left = buf[r, c, p, :, at - 128 : at].astype(F32)
                    else:
                        left = buf[before, c, p, :, width - 128 :].astype(F32) * has_before
                    both = pltpu.roll(jnp.where(lane < 64, right, left), 64 * half + 4 * i + 2, 1)
                    border = jnp.where(windows[half * PAIRS + i], both, border)
            out[x * NR + r, 2 * PAIRS] = border.astype(BF16)
        return 0

    lax.fori_loop(0, NR, column, 0)


def pack(images):
    return pl.pallas_call(
        pack_kernel,
        in_specs=[pl.BlockSpec(memory_space=pltpu.HBM)],
        out_specs=VMEM,
        out_shape=jax.ShapeDtypeStruct((NXD * NR, PIECE, 8, 128), BF16),
        scratch_shapes=[pltpu.VMEM((NR, COLOUR, ZP, 8, NXD * PT), BF16), pltpu.SemaphoreType.DMA((NR,))],
        compiler_params=params(16),
        cost_estimate=cost(2),
        name="pack_pieces",
    )(pltpu.with_memory_space_constraint(images, pltpu.HBM))


def prepare_kernel(labels, owners, counts, codebook, marks, cbt, bands):
    z, x, r = position()
    owner = owners[...]
    own = lax.broadcasted_iota(jnp.int32, (TILES, CELLS), 0) == owner
    own_f = jnp.where(own, 1.0, 0.0)
    earlier = lax.broadcasted_iota(jnp.int32, (CELLS, CELLS), 0) < lax.broadcasted_iota(jnp.int32, (CELLS, CELLS), 1)
    earlier = jnp.where(earlier, 1.0, 0.0).astype(BF16)
    ahead = jnp.dot(own_f.astype(BF16), earlier, preferred_element_type=F32)
    place = jnp.sum(own_f * ahead, axis=0, keepdims=True).astype(jnp.int32)
    cell = lax.broadcasted_iota(jnp.int32, (1, CELLS), 1)
    goes = jnp.where(cell < counts[NXD * z + x], owner * CAP + place, -1)
    for p in range(ZP):
        marks[p * ROWS : (p + 1) * ROWS] = labels[p]
    marks[ZP * ROWS :] = jnp.broadcast_to(goes, (8, CELLS))

    out_row = lax.broadcasted_iota(jnp.int32, (CH, CH), 0)
    in_row = lax.broadcasted_iota(jnp.int32, (CH, CH), 1)
    order = jnp.where(in_row == (out_row % NR) * COLOUR + out_row // NR, 1.0, 0.0).astype(BF16)
    wide = jnp.dot(order, codebook[...], preferred_element_type=F32) * (SOFTMAX_HEAT * LOG2E)
    flat = jnp.concatenate([wide, jnp.zeros((CH, GP - GENES), F32)], axis=1).T
    hi = flat.astype(BF16)
    mid = (flat - hi.astype(F32)).astype(BF16)
    lo = (flat - hi.astype(F32) - mid.astype(F32)).astype(BF16)
    gene = lax.broadcasted_iota(jnp.int32, (GP, 16), 0)
    which = lax.broadcasted_iota(jnp.int32, (GP, 16), 1)
    shut = jnp.where((gene >= GENES) & (which == 0), -3.0e38, 0.0).astype(BF16)
    cbt[...] = jnp.concatenate([hi, mid, lo, shut], axis=1)

    tile = NXD * r + x
    source = lax.broadcasted_iota(jnp.int32, (WIDE, HALF), 0)
    target = lax.broadcasted_iota(jnp.int32, (WIDE, HALF), 1)
    e = source - HALF
    side = e % 4
    beyond = jnp.where(side < 2, side - 2, HALF - 2 + side)
    at = jnp.where(source < HALF, source, jnp.where(e % 64 < 4 * PAIRS, beyond, 4 * WIDE))
    gap = jnp.abs(at - target)
    once = jnp.where(gap == 1, 1.0, 0.0).astype(BF16)
    for half in range(2):
        outer = (tile == TILES - 1) if half else (tile == 0)
        edge = jnp.where(at == (HALF - 1 if half else 0), jnp.where(outer, 1.0, 0.0), 0.0)
        bands[half, :, :HALF] = once
        bands[half, :, HALF:] = jnp.where(gap == 2, 1.0, jnp.where(gap == 0, 2.0 - edge, 0.0)).astype(BF16)


def prepare(labels, owners, counts, codebook):
    return pl.pallas_call(
        prepare_kernel,
        in_specs=[VMEM, VMEM, SMEM, VMEM],
        out_specs=[VMEM] * 3,
        out_shape=[
            jax.ShapeDtypeStruct((MARKS, CELLS), jnp.int32),
            jax.ShapeDtypeStruct((GP, 3 * CH + 16), BF16),
            jax.ShapeDtypeStruct((2, WIDE, 2 * HALF), BF16),
        ],
        compiler_params=params(16),
        cost_estimate=cost(2),
        name="prepare",
    )(labels, owners, counts, codebook)


def transposed_rows(half, src, rows, store):
    lane = lax.broadcasted_iota(jnp.int32, (CH, 128), 1)
    colour = lax.broadcasted_iota(jnp.int32, (CH, 128), 0) // NR

    def swapped(i):
        return jnp.swapaxes(jnp.stack([src(r, i) for r in range(NR)]).astype(F32), 0, 1)

    edge = swapped(2 * PAIRS)
    for p in range(ZP):
        parts = [swapped(half * PAIRS + ZP * c + p) for c in range(COLOUR)]
        mask = (lane // 4) == 16 * half + colour * ZP + p
        for row in rows:
            store(row, p, 0, jnp.concatenate([part[row] for part in parts], axis=0).astype(BF16))
            border = jnp.concatenate([edge[row]] * COLOUR, axis=0)
            store(row, p, 1, jnp.where(mask, border, 0.0).astype(BF16))


def normalise(value):
    mean = jnp.sum(value * value, axis=0, keepdims=True) * (1.0 / CH)
    return (value * lax.rsqrt(mean + 49.0 * NOISE_LEVEL)).astype(BF16)


def vertical(first, second, third):
    return 6.0 * second - (first + third)


def rows_at(start, size):
    return pl.ds(start if isinstance(start, int) else pl.multiple_of(start, 16), size)


def stencil_steps(half, g, bands, unit, last, xt, y, a_s, b_s):
    def regroup(k):
        base = k * 8 * STEP

        def store(row, p, t, block):
            xt[rows_at(base + (row * ZP + p) * CH, CH), t * 128 : (t + 1) * 128] = block

        transposed_rows(half, lambda r, i: g[k * NR + r, i], range(8), store)
        at = rows_at(base, 8 * STEP)
        y[at, :] = jnp.dot(xt[at, :], bands[half], preferred_element_type=F32)

    def keep():
        last[half] = xt[(ROWS - 4) * STEP :]

    def raw(row, p):
        return xt[rows_at(row * STEP + p * CH, CH), :HALF].astype(F32)

    def cols(row, p, twice):
        return y[rows_at(row * STEP + p * CH, CH), twice * HALF : (twice + 1) * HALF]

    def first(row):
        here = [raw(row, p) for p in range(ZP)]
        for p in range(ZP):
            cx = cols(row, p, 0)
            a = vertical(raw(row - 1, p), here[p], raw(row + 1, p)) - here[1 - p] - cx
            a_s[row, p] = a
            b_s[row, p] = a - cx

    def second(k):
        for odd in range(2):
            row = 2 * k + odd
            mid = [b_s[row, p] for p in range(ZP)]
            for p in range(ZP):
                mb = vertical(b_s[row - 1, p], mid[p], b_s[row + 1, p]) - mid[1 - p]
                at = (odd * ZP + p) * HALF
                unit[k, :, at : at + HALF] = normalise(a_s[row, p] + SHARPEN * (mb + cols(row, p, 1)))

    return regroup, keep, first, second


def loop(low, high, step):
    def body(k, _):
        step(k)
        return 0

    lax.fori_loop(low, high, body, 0)


def no_maximum_needed(codebook):
    wide = codebook[...].astype(F32)
    longest = jnp.max(jnp.sum(wide * wide, axis=0, keepdims=True))
    return longest * (CH * (1.01 * SOFTMAX_HEAT * LOG2E) ** 2) <= SAFE * SAFE


def posterior_steps(cbt, acc):
    slots = lax.broadcasted_iota(jnp.int32, (CELLS, VOX), 0).astype(F32).astype(BF16)

    def logits_of(u):
        stacked = jnp.concatenate([u, u, u, jnp.ones((16, VOX), BF16)], axis=0)
        return jnp.dot(cbt[...], stacked, preferred_element_type=F32)

    def add(post, label):
        onehot = jnp.where(slots == label.astype(F32).astype(BF16), jnp.ones((), BF16), jnp.zeros((), BF16))
        acc[...] += lax.dot_general(post, onehot, NT, preferred_element_type=F32)

    def begin(u, e_s):
        e = jnp.exp2(logits_of(u))
        e_s[...] = e
        return 1.0 / jnp.sum(e, axis=0, keepdims=True)

    def finish(inverse, label, e_s):
        add((e_s[...] * inverse).astype(BF16), label)

    def careful(u, label):
        logits = logits_of(u)
        e = jnp.exp2(logits - jnp.max(logits, axis=0, keepdims=True))
        add((e * (1.0 / jnp.sum(e, axis=0, keepdims=True))).astype(BF16), label)

    return begin, finish, careful


def label_row(marks, half, row):
    parts = [marks[pl.ds(p * ROWS + row + odd, 1), :] for odd in range(2) for p in range(ZP)]
    return jnp.concatenate([part[:, half * HALF : (half + 1) * HALF] for part in parts], axis=1)


def decode_kernel(g, bands, marks, cbt, codebook, acc, last, xt, y, a_s, b_s, unit0, unit1, e0, e1):
    units, buffers = (unit0, unit1), (e0, e1)
    acc[...] = jnp.zeros_like(acc)
    begin, finish, careful = posterior_steps(cbt, acc)
    halves = [stencil_steps(half, g, bands, units[half], last, xt, y, a_s, b_s) for half in range(2)]
    fine = no_maximum_needed(codebook)

    def label(half, k):
        return label_row(marks, half, 2 * k)

    def block(half, k):
        regroup, keep, first, second = halves[half]
        regroup(k)
        if k == ROWS // 8 - 1:
            keep()
        for row in range(max(8 * k - 1, 1), 8 * k + 7):
            first(row)
        pairs = list(range(max(4 * k - 1, 1), 4 * k + 3))
        for pair in pairs:
            second(pair)
        return [(half, pair) for pair in pairs]

    @pl.when(fine)
    def _():
        blocks = [(half, k) for half in range(2) for k in range(ROWS // 8)]
        ready = block(*blocks[0])
        started = None
        for number in range(len(blocks)):
            coming = block(*blocks[number + 1]) if number + 1 < len(blocks) else []
            for n, (half, pair) in enumerate(ready):
                if started is None:
                    started = (0, begin(units[half][pair], buffers[0]))
                slot, inverse = started
                following = (ready[n + 1 :] + coming)[:1]
                started = None
                for half2, pair2 in following:
                    started = (1 - slot, begin(units[half2][pair2], buffers[1 - slot]))
                finish(inverse, label(half, pair), buffers[slot])
            ready = coming

    @pl.when(jnp.logical_not(fine))
    def _():
        for half, (regroup, keep, first, second) in enumerate(halves):
            loop(0, ROWS // 8, regroup)
            keep()
            loop(1, ROWS - 1, first)
            loop(1, ROWS // 2 - 1, second)
            loop(1, ROWS // 2 - 1, lambda k: careful(units[half][k], label(half, k)))


def decode(g, bands, marks, cbt, codebook):
    return pl.pallas_call(
        decode_kernel,
        in_specs=[VMEM] * 5,
        out_specs=[VMEM] * 2,
        out_shape=[
            jax.ShapeDtypeStruct((GP, CELLS), F32),
            jax.ShapeDtypeStruct((2, 4 * STEP, WIDE), BF16),
        ],
        scratch_shapes=[
            pltpu.VMEM((ROWS * STEP, WIDE), BF16),
            pltpu.VMEM((ROWS * STEP, 2 * HALF), F32),
            pltpu.VMEM((ROWS, ZP, CH, HALF), F32),
            pltpu.VMEM((ROWS, ZP, CH, HALF), F32),
            pltpu.VMEM((ROWS // 2, CH, VOX), BF16),
            pltpu.VMEM((ROWS // 2, CH, VOX), BF16),
            pltpu.VMEM((GP, VOX), F32),
            pltpu.VMEM((GP, VOX), F32),
        ],
        compiler_params=params(36),
        cost_estimate=cost(15),
        name="decode_band",
    )(g, bands, marks, cbt, codebook)


def border_kernel(last, bands, following, marks, cbt, codebook, given, out, xh, ue, acc, e0, e1):
    joined = jnp.where(position()[0] < NZ - 1, 1.0, 0.0)

    def prepare_units():
        for half in range(2):
            xh[: 4 * STEP] = last[half]

            def store(row, p, t, block):
                start = (4 + row) * STEP + p * CH
                xh[start : start + CH, t * 128 : (t + 1) * 128] = block

            transposed_rows(half, lambda r, i: following[r * PIECE + i], range(4), store)
            y = jnp.dot(xh[STEP : 7 * STEP], bands[half], preferred_element_type=F32)

            def raw(row, p):
                return xh[row * STEP + p * CH : row * STEP + (p + 1) * CH, :HALF].astype(F32)

            def cols(row, p, twice):
                start = (row - 1) * STEP + p * CH
                return y[start : start + CH, twice * HALF : (twice + 1) * HALF]

            def up(get, row, p):
                return get(row - 1, p) * joined if row == 4 else get(row - 1, p)

            def down(get, row, p):
                return get(row + 1, p) * joined if row == 3 else get(row + 1, p)

            a, b = {}, {}
            for row in range(1, 7):
                for p in range(ZP):
                    cx = cols(row, p, 0)
                    a[row, p] = vertical(up(raw, row, p), raw(row, p), down(raw, row, p)) - raw(row, 1 - p) - cx
                    b[row, p] = a[row, p] - cx

            def get_b(row, p):
                return b[row, p]

            for row in range(2, 6):
                for p in range(ZP):
                    mb = vertical(up(get_b, row, p), b[row, p], down(get_b, row, p)) - b[row, 1 - p]
                    at = ((row % 2) * ZP + p) * HALF
                    ue[half * 2 + row // 2 - 1, :, at : at + HALF] = normalise(
                        a[row, p] + SHARPEN * (mb + cols(row, p, 1))
                    )

    acc[...] = given[...]
    tops = [following[NR * PIECE + h].astype(F32).astype(jnp.int32) for h in range(2)]

    def mark(k):
        own = [label_row(marks, h, ROWS - 2) for h in range(2)]
        next_ = [
            jnp.concatenate([tops[h][i : i + 1] for i in range(4)], axis=1) for h in range(2)
        ]
        return jnp.where(k < 2, jnp.where(k == 0, own[0], next_[0]), jnp.where(k == 2, own[1], next_[1]))

    begin, finish, careful = posterior_steps(cbt, acc)
    fine = no_maximum_needed(codebook)

    @pl.when(fine)
    def _():
        prepare_units()
        inv = begin(ue[0], e0)
        nxt = begin(ue[1], e1)
        finish(inv, mark(0), e0)
        inv = begin(ue[2], e0)
        finish(nxt, mark(1), e1)
        nxt = begin(ue[3], e1)
        finish(inv, mark(2), e0)
        finish(nxt, mark(3), e1)

    @pl.when(jnp.logical_not(fine))
    def _():
        prepare_units()
        loop(0, 4, lambda k: careful(ue[k], mark(k)))

    goes = marks[ZP * ROWS : ZP * ROWS + 1]
    select = jnp.where(lax.broadcasted_iota(jnp.int32, (TILES * CAP, CELLS), 0) == goes, SCALE, 0.0).astype(BF16)
    sums = jnp.concatenate([acc[...], jnp.zeros((128 * (FULL + 1) - GP, CELLS), F32)], axis=0)
    high = sums.astype(BF16)
    low = (sums - high.astype(F32)).astype(BF16)
    packed = lax.dot_general(select, high, NT, preferred_element_type=F32)
    packed = packed + lax.dot_general(select, low, NT, preferred_element_type=F32)
    lane = lax.broadcasted_iota(jnp.int32, (CAP // 2, 128), 1)
    for o in range(TILES):
        rows = packed[o * CAP : (o + 1) * CAP]
        for t in range(FULL):
            out[o, t * CAP : (t + 1) * CAP] = rows[:, t * 128 : (t + 1) * 128]
        rest = rows[:, FULL * 128 :]
        out[o, FULL * CAP :] = jnp.where(lane < 64, rest[: CAP // 2], pltpu.roll(rest[CAP // 2 :], 64, 1))


def border(last, bands, following, marks, cbt, codebook, given):
    return pl.pallas_call(
        border_kernel,
        in_specs=[VMEM] * 7,
        out_specs=VMEM,
        out_shape=jax.ShapeDtypeStruct((TILES, OUT_ROWS, 128), F32),
        scratch_shapes=[
            pltpu.VMEM((8 * STEP, WIDE), BF16),
            pltpu.VMEM((4, CH, VOX), BF16),
            pltpu.VMEM((GP, CELLS), F32),
            pltpu.VMEM((GP, VOX), F32),
            pltpu.VMEM((GP, VOX), F32),
        ],
        compiler_params=params(24),
        cost_estimate=cost(4),
        name="border_rows",
    )(last, bands, following, marks, cbt, codebook, given)


def unpack_kernel(parts, out):
    half_rounds = NR // 2
    y = lax.axis_index("y")
    for core in range(2):
        for back in range(half_rounds):
            r = 2 * ((y + half_rounds - back) % half_rounds) + core
            for x in range(NXD):
                src, dst = (core * half_rounds + back) * NXD + x, NXD * r + x
                for t in range(FULL):
                    out[0, dst, :, t * 128 : (t + 1) * 128] = parts[src, t * CAP : (t + 1) * CAP] * (1.0 / SCALE)
                rest = parts[src, FULL * CAP :] * (1.0 / SCALE)
                out[0, dst, : CAP // 2, FULL * 128 :] = rest[:, :REST]
                out[0, dst, CAP // 2 :, FULL * 128 :] = pltpu.roll(rest, 64, 1)[:, :REST]


def unpack(parts):
    return pl.pallas_call(
        unpack_kernel,
        in_specs=[VMEM],
        out_specs=VMEM,
        out_shape=jax.ShapeDtypeStruct((1, TILES, CAP, GENES), F32),
        compiler_params=params(16),
        name="unpack_cells",
    )(parts)


def local(images, labels, counts, owners, codebook):
    swap = [
        (z * NXD * NR + x * NR + r, r * NXD * NR + x * NR + z)
        for z in range(NZ)
        for x in range(NXD)
        for r in range(NR)
    ]
    exchange = functools.partial(lax.all_to_all, split_axis=0, concat_axis=0, tiled=True)
    g = exchange(pack(images), ("x", "y", "c"))
    marks, cbt, bands = prepare(labels, owners.reshape(1, CELLS), counts, codebook)
    marks = lax.ppermute(marks, ("z", "x", "y", "c"), swap)
    tops = marks[: ZP * ROWS].reshape(ZP, ROWS, 2, HALF)[:, :2].transpose(2, 1, 0, 3).reshape(2, 4, HALF)
    upper = jnp.concatenate([g[:NR, :, :4].reshape(NR * PIECE, 4, 128), tops.astype(BF16)], axis=0)
    following = lax.ppermute(upper, "z", [((i + 1) % NZ, i) for i in range(NZ)])
    acc, last = decode(g, bands, marks, cbt, codebook)
    packed = border(last, bands, following, marks, cbt, codebook, acc)
    parts = exchange(packed.astype(jnp.float16), ("z", "x")).reshape(NZ, NXD, OUT_ROWS, 128)
    summed = jnp.sum(parts.astype(F32), axis=0).astype(jnp.float16)
    ring = NR // 2
    hops = [lax.ppermute(summed, "y", [(i, (i + k) % ring) for i in range(ring)]) for k in range(1, ring)]
    received = lax.all_gather(jnp.concatenate([summed, *hops], axis=0), "c", tiled=True)
    return unpack(received.astype(F32))


def solution(mesh):
    grid = Mesh(mesh.devices.reshape(NZ, NXD, NR // 2, 2), ("z", "x", "y", "c"))
    rounds = ("y", "c")
    in_specs = (P(rounds, None, ("z", "x"), None), P(None, rounds, ("z", "x")), P(), P(("z", "x"), None), P())
    out_specs = P(("z", "x"), None, None, None)
    return jax.shard_map(local, mesh=grid, in_specs=in_specs, out_specs=out_specs, check_vma=False)
```

```python
import functools

import jax
import jax.numpy as jnp
from jax import lax
from jax.experimental import pallas as pl
from jax.experimental.pallas import tpu as pltpu
from jax.sharding import Mesh, PartitionSpec as P

SOFTMAX_HEAT = 0.6
SHARPEN = 0.15
NOISE_LEVEL = 1.0
LOG2E = 1.4426950408889634

CH, GENES, ZP, PT, CELLS, TILES, CAP = 48, 550, 2, 256, 256, 32, 16
NZ, NXD, NR = 8, 4, 8
GP = 552
COLOUR = CH // NR
PAIRS = COLOUR * ZP
HALF = PT // 2
PIECE = 2 * PAIRS + 1
ROWS = 32
STEP = ZP * CH
WIDE = HALF + 128
VOX = 2 * ZP * HALF
MARKS = ZP * ROWS + 8
FULL = GENES // 128
REST = GENES - 128 * FULL
OUT_ROWS = FULL * CAP + CAP // 2
SCALE = 0.25
SAFE = 100.0
F32, BF16 = jnp.float32, jnp.bfloat16
NT = (((1,), (1,)), ((), ()))
VMEM = pl.BlockSpec(memory_space=pltpu.VMEM)
SMEM = pl.BlockSpec(memory_space=pltpu.SMEM)
MIB = 1024 * 1024


def position():
    return lax.axis_index("z"), lax.axis_index("x"), 2 * lax.axis_index("y") + lax.axis_index("c")


def params(mib):
    return pltpu.CompilerParams(vmem_limit_bytes=mib * MIB)


def cost(us):
    return pl.CostEstimate(flops=int(us * 1e9), bytes_accessed=int(us * 3e6), transcendentals=0)


def pack_kernel(img, out, buf, sems):
    lane = lax.broadcasted_iota(jnp.int32, (8, 128), 1)
    windows = [(lane // 4) == 16 * half + i for half in range(2) for i in range(PAIRS)]
    width = NXD * PT

    def fetch(r):
        start = pl.multiple_of(r * width, width)
        return pltpu.make_async_copy(img.at[:, :, :, pl.ds(start, width)], buf.at[r], sems.at[r])

    for r in range(NR):
        fetch(r).start()
    fetch(0).wait()

    def column(r, _):
        after, before = jnp.minimum(r + 1, NR - 1), jnp.maximum(r - 1, 0)

        @pl.when(r < NR - 1)
        def _():
            fetch(after).wait()

        has_after, has_before = (r < NR - 1).astype(F32), (r > 0).astype(F32)
        for x in range(NXD):
            border = jnp.zeros((8, 128), F32)
            for half in range(2):
                at = PT * x + HALF * half
                for i in range(PAIRS):
                    c, p = i // ZP, i % ZP
                    out[x * NR + r, half * PAIRS + i] = buf[r, c, p, :, at : at + HALF]
                    if at + HALF < width:
                        right = buf[r, c, p, :, at + HALF : at + 2 * HALF].astype(F32)
                    else:
                        right = buf[after, c, p, :, :128].astype(F32) * has_after
                    if at > 0:
                        left = buf[r, c, p, :, at - 128 : at].astype(F32)
                    else:
                        left = buf[before, c, p, :, width - 128 :].astype(F32) * has_before
                    both = pltpu.roll(jnp.where(lane < 64, right, left), 64 * half + 4 * i + 2, 1)
                    border = jnp.where(windows[half * PAIRS + i], both, border)
            out[x * NR + r, 2 * PAIRS] = border.astype(BF16)
        return 0

    lax.fori_loop(0, NR, column, 0)


def pack(images):
    return pl.pallas_call(
        pack_kernel,
        in_specs=[pl.BlockSpec(memory_space=pltpu.HBM)],
        out_specs=VMEM,
        out_shape=jax.ShapeDtypeStruct((NXD * NR, PIECE, 8, 128), BF16),
        scratch_shapes=[pltpu.VMEM((NR, COLOUR, ZP, 8, NXD * PT), BF16), pltpu.SemaphoreType.DMA((NR,))],
        compiler_params=params(16),
        cost_estimate=cost(2),
        name="pack_pieces",
    )(pltpu.with_memory_space_constraint(images, pltpu.HBM))


def prepare_kernel(labels, owners, counts, codebook, marks, cbt, bands):
    z, x, r = position()
    owner = owners[...]
    own = lax.broadcasted_iota(jnp.int32, (TILES, CELLS), 0) == owner
    own_f = jnp.where(own, 1.0, 0.0)
    earlier = lax.broadcasted_iota(jnp.int32, (CELLS, CELLS), 0) < lax.broadcasted_iota(jnp.int32, (CELLS, CELLS), 1)
    earlier = jnp.where(earlier, 1.0, 0.0).astype(BF16)
    ahead = jnp.dot(own_f.astype(BF16), earlier, preferred_element_type=F32)
    place = jnp.sum(own_f * ahead, axis=0, keepdims=True).astype(jnp.int32)
    cell = lax.broadcasted_iota(jnp.int32, (1, CELLS), 1)
    goes = jnp.where(cell < counts[NXD * z + x], owner * CAP + place, -1)
    for p in range(ZP):
        marks[p * ROWS : (p + 1) * ROWS] = labels[p]
    marks[ZP * ROWS :] = jnp.broadcast_to(goes, (8, CELLS))

    out_row = lax.broadcasted_iota(jnp.int32, (CH, CH), 0)
    in_row = lax.broadcasted_iota(jnp.int32, (CH, CH), 1)
    order = jnp.where(in_row == (out_row % NR) * COLOUR + out_row // NR, 1.0, 0.0).astype(BF16)
    wide = jnp.dot(order, codebook[...], preferred_element_type=F32) * (SOFTMAX_HEAT * LOG2E)
    flat = jnp.concatenate([wide, jnp.zeros((CH, GP - GENES), F32)], axis=1).T
    hi = flat.astype(BF16)
    mid = (flat - hi.astype(F32)).astype(BF16)
    lo = (flat - hi.astype(F32) - mid.astype(F32)).astype(BF16)
    gene = lax.broadcasted_iota(jnp.int32, (GP, 16), 0)
    which = lax.broadcasted_iota(jnp.int32, (GP, 16), 1)
    shut = jnp.where((gene >= GENES) & (which == 0), -3.0e38, 0.0).astype(BF16)
    cbt[...] = jnp.concatenate([hi, mid, lo, shut], axis=1)

    tile = NXD * r + x
    source = lax.broadcasted_iota(jnp.int32, (WIDE, HALF), 0)
    target = lax.broadcasted_iota(jnp.int32, (WIDE, HALF), 1)
    e = source - HALF
    side = e % 4
    beyond = jnp.where(side < 2, side - 2, HALF - 2 + side)
    at = jnp.where(source < HALF, source, jnp.where(e % 64 < 4 * PAIRS, beyond, 4 * WIDE))
    gap = jnp.abs(at - target)
    once = jnp.where(gap == 1, 1.0, 0.0).astype(BF16)
    for half in range(2):
        outer = (tile == TILES - 1) if half else (tile == 0)
        edge = jnp.where(at == (HALF - 1 if half else 0), jnp.where(outer, 1.0, 0.0), 0.0)
        bands[half, :, :HALF] = once
        bands[half, :, HALF:] = jnp.where(gap == 2, 1.0, jnp.where(gap == 0, 2.0 - edge, 0.0)).astype(BF16)


def prepare(labels, owners, counts, codebook):
    return pl.pallas_call(
        prepare_kernel,
        in_specs=[VMEM, VMEM, SMEM, VMEM],
        out_specs=[VMEM] * 3,
        out_shape=[
            jax.ShapeDtypeStruct((MARKS, CELLS), jnp.int32),
            jax.ShapeDtypeStruct((GP, 3 * CH + 16), BF16),
            jax.ShapeDtypeStruct((2, WIDE, 2 * HALF), BF16),
        ],
        compiler_params=params(16),
        cost_estimate=cost(2),
        name="prepare",
    )(labels, owners, counts, codebook)


def transposed_rows(half, src, rows, store):
    lane = lax.broadcasted_iota(jnp.int32, (CH, 128), 1)
    colour = lax.broadcasted_iota(jnp.int32, (CH, 128), 0) // NR

    def swapped(i):
        return jnp.swapaxes(jnp.stack([src(r, i) for r in range(NR)]).astype(F32), 0, 1)

    edge = swapped(2 * PAIRS)
    for p in range(ZP):
        parts = [swapped(half * PAIRS + ZP * c + p) for c in range(COLOUR)]
        mask = (lane // 4) == 16 * half + colour * ZP + p
        for row in rows:
            store(row, p, 0, jnp.concatenate([part[row] for part in parts], axis=0).astype(BF16))
            border = jnp.concatenate([edge[row]] * COLOUR, axis=0)
            store(row, p, 1, jnp.where(mask, border, 0.0).astype(BF16))


def normalise(value):
    mean = jnp.sum(value * value, axis=0, keepdims=True) * (1.0 / CH)
    return (value * lax.rsqrt(mean + 49.0 * NOISE_LEVEL)).astype(BF16)


def vertical(first, second, third):
    return 6.0 * second - (first + third)


def rows_at(start, size):
    return pl.ds(start if isinstance(start, int) else pl.multiple_of(start, 16), size)


def stencil_steps(half, g, bands, unit, last, xt, y, a_s, b_s):
    def regroup(k):
        base = k * 8 * STEP

        def store(row, p, t, block):
            xt[rows_at(base + (row * ZP + p) * CH, CH), t * 128 : (t + 1) * 128] = block

        transposed_rows(half, lambda r, i: g[k * NR + r, i], range(8), store)
        at = rows_at(base, 8 * STEP)
        y[at, :] = jnp.dot(xt[at, :], bands[half], preferred_element_type=F32)

    def keep():
        last[half] = xt[(ROWS - 4) * STEP :]

    def raw(row, p):
        return xt[rows_at(row * STEP + p * CH, CH), :HALF].astype(F32)

    def cols(row, p, twice):
        return y[rows_at(row * STEP + p * CH, CH), twice * HALF : (twice + 1) * HALF]

    def first(row):
        here = [raw(row, p) for p in range(ZP)]
        for p in range(ZP):
            cx = cols(row, p, 0)
            a = vertical(raw(row - 1, p), here[p], raw(row + 1, p)) - here[1 - p] - cx
            a_s[row, p] = a
            b_s[row, p] = a - cx

    def second(k):
        for odd in range(2):
            row = 2 * k + odd
            mid = [b_s[row, p] for p in range(ZP)]
            for p in range(ZP):
                mb = vertical(b_s[row - 1, p], mid[p], b_s[row + 1, p]) - mid[1 - p]
                at = (odd * ZP + p) * HALF
                unit[k, :, at : at + HALF] = normalise(a_s[row, p] + SHARPEN * (mb + cols(row, p, 1)))

    return regroup, keep, first, second


def loop(low, high, step):
    def body(k, _):
        step(k)
        return 0

    lax.fori_loop(low, high, body, 0)


def no_maximum_needed(codebook):
    wide = codebook[...].astype(F32)
    longest = jnp.max(jnp.sum(wide * wide, axis=0, keepdims=True))
    return longest * (CH * (1.01 * SOFTMAX_HEAT * LOG2E) ** 2) <= SAFE * SAFE


def posterior_steps(cbt, acc):
    slots = lax.broadcasted_iota(jnp.int32, (CELLS, VOX), 0).astype(F32).astype(BF16)

    def logits_of(u):
        stacked = jnp.concatenate([u, u, u, jnp.ones((16, VOX), BF16)], axis=0)
        return jnp.dot(cbt[...], stacked, preferred_element_type=F32)

    def add(post, label):
        onehot = jnp.where(slots == label.astype(F32).astype(BF16), jnp.ones((), BF16), jnp.zeros((), BF16))
        acc[...] += lax.dot_general(post, onehot, NT, preferred_element_type=F32)

    def begin(u, e_s):
        e = jnp.exp2(logits_of(u))
        e_s[...] = e
        return 1.0 / jnp.sum(e, axis=0, keepdims=True)

    def finish(inverse, label, e_s):
        add((e_s[...] * inverse).astype(BF16), label)

    def careful(u, label):
        logits = logits_of(u)
        e = jnp.exp2(logits - jnp.max(logits, axis=0, keepdims=True))
        add((e * (1.0 / jnp.sum(e, axis=0, keepdims=True))).astype(BF16), label)

    return begin, finish, careful


def label_row(marks, half, row):
    parts = [marks[pl.ds(p * ROWS + row + odd, 1), :] for odd in range(2) for p in range(ZP)]
    return jnp.concatenate([part[:, half * HALF : (half + 1) * HALF] for part in parts], axis=1)


def decode_kernel(g, bands, marks, cbt, codebook, acc, last, xt, y, a_s, b_s, unit0, unit1, e0, e1):
    units, buffers = (unit0, unit1), (e0, e1)
    acc[...] = jnp.zeros_like(acc)
    begin, finish, careful = posterior_steps(cbt, acc)
    halves = [stencil_steps(half, g, bands, units[half], last, xt, y, a_s, b_s) for half in range(2)]
    fine = no_maximum_needed(codebook)

    def label(half, k):
        return label_row(marks, half, 2 * k)

    def block(half, k):
        regroup, keep, first, second = halves[half]
        regroup(k)
        if k == ROWS // 8 - 1:
            keep()
        for row in range(max(8 * k - 1, 1), 8 * k + 7):
            first(row)
        pairs = list(range(max(4 * k - 1, 1), 4 * k + 3))
        for pair in pairs:
            second(pair)
        return [(half, pair) for pair in pairs]

    @pl.when(fine)
    def _():
        blocks = [(half, k) for half in range(2) for k in range(ROWS // 8)]
        ready = block(*blocks[0])
        started = None
        for number in range(len(blocks)):
            coming = block(*blocks[number + 1]) if number + 1 < len(blocks) else []
            for n, (half, pair) in enumerate(ready):
                if started is None:
                    started = (0, begin(units[half][pair], buffers[0]))
                slot, inverse = started
                following = (ready[n + 1 :] + coming)[:1]
                started = None
                for half2, pair2 in following:
                    started = (1 - slot, begin(units[half2][pair2], buffers[1 - slot]))
                finish(inverse, label(half, pair), buffers[slot])
            ready = coming

    @pl.when(jnp.logical_not(fine))
    def _():
        for half, (regroup, keep, first, second) in enumerate(halves):
            loop(0, ROWS // 8, regroup)
            keep()
            loop(1, ROWS - 1, first)
            loop(1, ROWS // 2 - 1, second)
            loop(1, ROWS // 2 - 1, lambda k: careful(units[half][k], label(half, k)))


def decode(g, bands, marks, cbt, codebook):
    return pl.pallas_call(
        decode_kernel,
        in_specs=[VMEM] * 5,
        out_specs=[VMEM] * 2,
        out_shape=[
            jax.ShapeDtypeStruct((GP, CELLS), F32),
            jax.ShapeDtypeStruct((2, 4 * STEP, WIDE), BF16),
        ],
        scratch_shapes=[
            pltpu.VMEM((ROWS * STEP, WIDE), BF16),
            pltpu.VMEM((ROWS * STEP, 2 * HALF), F32),
            pltpu.VMEM((ROWS, ZP, CH, HALF), F32),
            pltpu.VMEM((ROWS, ZP, CH, HALF), F32),
            pltpu.VMEM((ROWS // 2, CH, VOX), BF16),
            pltpu.VMEM((ROWS // 2, CH, VOX), BF16),
            pltpu.VMEM((GP, VOX), F32),
            pltpu.VMEM((GP, VOX), F32),
        ],
        compiler_params=params(36),
        cost_estimate=cost(15),
        name="decode_band",
    )(g, bands, marks, cbt, codebook)


def border_kernel(last, bands, following, marks, cbt, codebook, given, out, xh, ue, acc, e0, e1):
    joined = jnp.where(position()[0] < NZ - 1, 1.0, 0.0)

    def prepare_units():
        for half in range(2):
            xh[: 4 * STEP] = last[half]

            def store(row, p, t, block):
                start = (4 + row) * STEP + p * CH
                xh[start : start + CH, t * 128 : (t + 1) * 128] = block

            transposed_rows(half, lambda r, i: following[r * PIECE + i], range(4), store)
            y = jnp.dot(xh[STEP : 7 * STEP], bands[half], preferred_element_type=F32)

            def raw(row, p):
                return xh[row * STEP + p * CH : row * STEP + (p + 1) * CH, :HALF].astype(F32)

            def cols(row, p, twice):
                start = (row - 1) * STEP + p * CH
                return y[start : start + CH, twice * HALF : (twice + 1) * HALF]

            def up(get, row, p):
                return get(row - 1, p) * joined if row == 4 else get(row - 1, p)

            def down(get, row, p):
                return get(row + 1, p) * joined if row == 3 else get(row + 1, p)

            a, b = {}, {}
            for row in range(1, 7):
                for p in range(ZP):
                    cx = cols(row, p, 0)
                    a[row, p] = vertical(up(raw, row, p), raw(row, p), down(raw, row, p)) - raw(row, 1 - p) - cx
                    b[row, p] = a[row, p] - cx

            def get_b(row, p):
                return b[row, p]

            for row in range(2, 6):
                for p in range(ZP):
                    mb = vertical(up(get_b, row, p), b[row, p], down(get_b, row, p)) - b[row, 1 - p]
                    at = ((row % 2) * ZP + p) * HALF
                    ue[half * 2 + row // 2 - 1, :, at : at + HALF] = normalise(
                        a[row, p] + SHARPEN * (mb + cols(row, p, 1))
                    )

    acc[...] = given[...]
    tops = [following[NR * PIECE + h].astype(F32).astype(jnp.int32) for h in range(2)]

    def mark(k):
        own = [label_row(marks, h, ROWS - 2) for h in range(2)]
        next_ = [
            jnp.concatenate([tops[h][i : i + 1] for i in range(4)], axis=1) for h in range(2)
        ]
        return jnp.where(k < 2, jnp.where(k == 0, own[0], next_[0]), jnp.where(k == 2, own[1], next_[1]))

    begin, finish, careful = posterior_steps(cbt, acc)
    fine = no_maximum_needed(codebook)

    @pl.when(fine)
    def _():
        prepare_units()
        inv = begin(ue[0], e0)
        nxt = begin(ue[1], e1)
        finish(inv, mark(0), e0)
        inv = begin(ue[2], e0)
        finish(nxt, mark(1), e1)
        nxt = begin(ue[3], e1)
        finish(inv, mark(2), e0)
        finish(nxt, mark(3), e1)

    @pl.when(jnp.logical_not(fine))
    def _():
        prepare_units()
        loop(0, 4, lambda k: careful(ue[k], mark(k)))

    goes = marks[ZP * ROWS : ZP * ROWS + 1]
    select = jnp.where(lax.broadcasted_iota(jnp.int32, (TILES * CAP, CELLS), 0) == goes, SCALE, 0.0).astype(BF16)
    sums = jnp.concatenate([acc[...], jnp.zeros((128 * (FULL + 1) - GP, CELLS), F32)], axis=0)
    high = sums.astype(BF16)
    low = (sums - high.astype(F32)).astype(BF16)
    packed = lax.dot_general(select, high, NT, preferred_element_type=F32)
    packed = packed + lax.dot_general(select, low, NT, preferred_element_type=F32)
    lane = lax.broadcasted_iota(jnp.int32, (CAP // 2, 128), 1)
    for o in range(TILES):
        rows = packed[o * CAP : (o + 1) * CAP]
        for t in range(FULL):
            out[o, t * CAP : (t + 1) * CAP] = rows[:, t * 128 : (t + 1) * 128]
        rest = rows[:, FULL * 128 :]
        out[o, FULL * CAP :] = jnp.where(lane < 64, rest[: CAP // 2], pltpu.roll(rest[CAP // 2 :], 64, 1))


def border(last, bands, following, marks, cbt, codebook, given):
    return pl.pallas_call(
        border_kernel,
        in_specs=[VMEM] * 7,
        out_specs=VMEM,
        out_shape=jax.ShapeDtypeStruct((TILES, OUT_ROWS, 128), F32),
        scratch_shapes=[
            pltpu.VMEM((8 * STEP, WIDE), BF16),
            pltpu.VMEM((4, CH, VOX), BF16),
            pltpu.VMEM((GP, CELLS), F32),
            pltpu.VMEM((GP, VOX), F32),
            pltpu.VMEM((GP, VOX), F32),
        ],
        compiler_params=params(24),
        cost_estimate=cost(4),
        name="border_rows",
    )(last, bands, following, marks, cbt, codebook, given)


def unpack_kernel(parts, out):
    half_rounds = NR // 2
    y, c = lax.axis_index("y"), lax.axis_index("c")
    for other in range(2):
        for back in range(half_rounds):
            r = 2 * ((y + half_rounds - back) % half_rounds) + (c + other) % 2
            for x in range(NXD):
                src, dst = (other * half_rounds + back) * NXD + x, NXD * r + x
                for t in range(FULL):
                    out[0, dst, :, t * 128 : (t + 1) * 128] = parts[src, t * CAP : (t + 1) * CAP] * (1.0 / SCALE)
                rest = parts[src, FULL * CAP :] * (1.0 / SCALE)
                out[0, dst, : CAP // 2, FULL * 128 :] = rest[:, :REST]
                out[0, dst, CAP // 2 :, FULL * 128 :] = pltpu.roll(rest, 64, 1)[:, :REST]


def unpack(parts):
    return pl.pallas_call(
        unpack_kernel,
        in_specs=[VMEM],
        out_specs=VMEM,
        out_shape=jax.ShapeDtypeStruct((1, TILES, CAP, GENES), F32),
        compiler_params=params(16),
        name="unpack_cells",
    )(parts)


def local(images, labels, counts, owners, codebook):
    swap = [
        (z * NXD * NR + x * NR + r, r * NXD * NR + x * NR + z)
        for z in range(NZ)
        for x in range(NXD)
        for r in range(NR)
    ]
    exchange = functools.partial(lax.all_to_all, split_axis=0, concat_axis=0, tiled=True)
    g = exchange(pack(images), ("x", "y", "c"))
    marks, cbt, bands = prepare(labels, owners.reshape(1, CELLS), counts, codebook)
    marks = lax.ppermute(marks, ("z", "x", "y", "c"), swap)
    tops = marks[: ZP * ROWS].reshape(ZP, ROWS, 2, HALF)[:, :2].transpose(2, 1, 0, 3).reshape(2, 4, HALF)
    upper = jnp.concatenate([g[:NR, :, :4].reshape(NR * PIECE, 4, 128), tops.astype(BF16)], axis=0)
    following = lax.ppermute(upper, "z", [((i + 1) % NZ, i) for i in range(NZ)])
    acc, last = decode(g, bands, marks, cbt, codebook)
    packed = border(last, bands, following, marks, cbt, codebook, acc)
    parts = exchange(packed.astype(jnp.float16), ("z", "x")).reshape(NZ, NXD, OUT_ROWS, 128)
    summed = jnp.sum(parts.astype(F32), axis=0).astype(jnp.float16)
    ring = NR // 2
    hops = [lax.ppermute(summed, "y", [(i, (i + k) % ring) for i in range(ring)]) for k in range(1, ring)]
    own = [summed, *hops]
    others = [lax.ppermute(piece, "c", [(0, 1), (1, 0)]) for piece in own]
    received = jnp.concatenate(own + others, axis=0)
    return unpack(received.astype(F32))


def solution(mesh):
    grid = Mesh(mesh.devices.reshape(NZ, NXD, NR // 2, 2), ("z", "x", "y", "c"))
    rounds = ("y", "c")
    in_specs = (P(rounds, None, ("z", "x"), None), P(None, rounds, ("z", "x")), P(), P(("z", "x"), None), P())
    out_specs = P(("z", "x"), None, None, None)
    return jax.shard_map(local, mesh=grid, in_specs=in_specs, out_specs=out_specs, check_vma=False)
```

```python
import functools

import jax
import jax.numpy as jnp
from jax import lax
from jax.experimental import pallas as pl
from jax.experimental.pallas import tpu as pltpu
from jax.sharding import Mesh, PartitionSpec as P

SOFTMAX_HEAT = 0.6
SHARPEN = 0.15
NOISE_LEVEL = 1.0
LOG2E = 1.4426950408889634

CH, GENES, ZP, PT, CELLS, TILES, CAP = 48, 550, 2, 256, 256, 32, 16
NZ, NXD, NR = 8, 4, 8
GP = 552
COLOUR = CH // NR
PAIRS = COLOUR * ZP
HALF = PT // 2
PIECE = 2 * PAIRS + 1
ROWS = 32
STEP = ZP * CH
WIDE = HALF + 128
VOX = 2 * ZP * HALF
MARKS = ZP * ROWS + 8
FULL = GENES // 128
REST = GENES - 128 * FULL
OUT_ROWS = FULL * CAP + CAP // 2
SCALE = 0.25
SAFE = 100.0
F32, BF16 = jnp.float32, jnp.bfloat16
NT = (((1,), (1,)), ((), ()))
VMEM = pl.BlockSpec(memory_space=pltpu.VMEM)
SMEM = pl.BlockSpec(memory_space=pltpu.SMEM)
MIB = 1024 * 1024


def position():
    return lax.axis_index("z"), lax.axis_index("x"), 2 * lax.axis_index("y") + lax.axis_index("c")


def params(mib):
    return pltpu.CompilerParams(vmem_limit_bytes=mib * MIB)


def cost(us):
    return pl.CostEstimate(flops=int(us * 1e9), bytes_accessed=int(us * 3e6), transcendentals=0)


def pack_kernel(img, out, buf, sems):
    lane = lax.broadcasted_iota(jnp.int32, (8, 128), 1)
    windows = [(lane // 4) == 16 * half + i for half in range(2) for i in range(PAIRS)]
    width = NXD * PT

    def fetch(r):
        start = pl.multiple_of(r * width, width)
        return pltpu.make_async_copy(img.at[:, :, :, pl.ds(start, width)], buf.at[r], sems.at[r])

    for r in range(NR):
        fetch(r).start()
    fetch(0).wait()

    def column(r, _):
        after, before = jnp.minimum(r + 1, NR - 1), jnp.maximum(r - 1, 0)

        @pl.when(r < NR - 1)
        def _():
            fetch(after).wait()

        has_after, has_before = (r < NR - 1).astype(F32), (r > 0).astype(F32)
        for x in range(NXD):
            border = jnp.zeros((8, 128), F32)
            for half in range(2):
                at = PT * x + HALF * half
                for i in range(PAIRS):
                    c, p = i // ZP, i % ZP
                    out[x * NR + r, half * PAIRS + i] = buf[r, c, p, :, at : at + HALF]
                    if at + HALF < width:
                        right = buf[r, c, p, :, at + HALF : at + 2 * HALF].astype(F32)
                    else:
                        right = buf[after, c, p, :, :128].astype(F32) * has_after
                    if at > 0:
                        left = buf[r, c, p, :, at - 128 : at].astype(F32)
                    else:
                        left = buf[before, c, p, :, width - 128 :].astype(F32) * has_before
                    both = pltpu.roll(jnp.where(lane < 64, right, left), 64 * half + 4 * i + 2, 1)
                    border = jnp.where(windows[half * PAIRS + i], both, border)
            out[x * NR + r, 2 * PAIRS] = border.astype(BF16)
        return 0

    lax.fori_loop(0, NR, column, 0)


def pack(images):
    return pl.pallas_call(
        pack_kernel,
        in_specs=[pl.BlockSpec(memory_space=pltpu.HBM)],
        out_specs=VMEM,
        out_shape=jax.ShapeDtypeStruct((NXD * NR, PIECE, 8, 128), BF16),
        scratch_shapes=[pltpu.VMEM((NR, COLOUR, ZP, 8, NXD * PT), BF16), pltpu.SemaphoreType.DMA((NR,))],
        compiler_params=params(16),
        cost_estimate=cost(2),
        name="pack_pieces",
    )(pltpu.with_memory_space_constraint(images, pltpu.HBM))


def prepare_kernel(labels, owners, counts, codebook, marks, cbt, bands):
    z, x, r = position()
    owner = owners[...]
    own = lax.broadcasted_iota(jnp.int32, (TILES, CELLS), 0) == owner
    own_f = jnp.where(own, 1.0, 0.0)
    earlier = lax.broadcasted_iota(jnp.int32, (CELLS, CELLS), 0) < lax.broadcasted_iota(jnp.int32, (CELLS, CELLS), 1)
    earlier = jnp.where(earlier, 1.0, 0.0).astype(BF16)
    ahead = jnp.dot(own_f.astype(BF16), earlier, preferred_element_type=F32)
    place = jnp.sum(own_f * ahead, axis=0, keepdims=True).astype(jnp.int32)
    cell = lax.broadcasted_iota(jnp.int32, (1, CELLS), 1)
    goes = jnp.where(cell < counts[NXD * z + x], owner * CAP + place, -1)
    for p in range(ZP):
        marks[p * ROWS : (p + 1) * ROWS] = labels[p]
    marks[ZP * ROWS :] = jnp.broadcast_to(goes, (8, CELLS))

    out_row = lax.broadcasted_iota(jnp.int32, (CH, CH), 0)
    in_row = lax.broadcasted_iota(jnp.int32, (CH, CH), 1)
    order = jnp.where(in_row == (out_row % NR) * COLOUR + out_row // NR, 1.0, 0.0).astype(BF16)
    wide = jnp.dot(order, codebook[...], preferred_element_type=F32) * (SOFTMAX_HEAT * LOG2E)
    flat = jnp.concatenate([wide, jnp.zeros((CH, GP - GENES), F32)], axis=1).T
    hi = flat.astype(BF16)
    mid = (flat - hi.astype(F32)).astype(BF16)
    lo = (flat - hi.astype(F32) - mid.astype(F32)).astype(BF16)
    gene = lax.broadcasted_iota(jnp.int32, (GP, 16), 0)
    which = lax.broadcasted_iota(jnp.int32, (GP, 16), 1)
    shut = jnp.where((gene >= GENES) & (which == 0), -3.0e38, 0.0).astype(BF16)
    cbt[...] = jnp.concatenate([hi, mid, lo, shut], axis=1)

    tile = NXD * r + x
    source = lax.broadcasted_iota(jnp.int32, (WIDE, HALF), 0)
    target = lax.broadcasted_iota(jnp.int32, (WIDE, HALF), 1)
    e = source - HALF
    side = e % 4
    beyond = jnp.where(side < 2, side - 2, HALF - 2 + side)
    at = jnp.where(source < HALF, source, jnp.where(e % 64 < 4 * PAIRS, beyond, 4 * WIDE))
    gap = jnp.abs(at - target)
    once = jnp.where(gap == 1, 1.0, 0.0).astype(BF16)
    for half in range(2):
        outer = (tile == TILES - 1) if half else (tile == 0)
        edge = jnp.where(at == (HALF - 1 if half else 0), jnp.where(outer, 1.0, 0.0), 0.0)
        bands[half, :, :HALF] = once
        bands[half, :, HALF:] = jnp.where(gap == 2, 1.0, jnp.where(gap == 0, 2.0 - edge, 0.0)).astype(BF16)


def prepare(labels, owners, counts, codebook):
    return pl.pallas_call(
        prepare_kernel,
        in_specs=[VMEM, VMEM, SMEM, VMEM],
        out_specs=[VMEM] * 3,
        out_shape=[
            jax.ShapeDtypeStruct((MARKS, CELLS), jnp.int32),
            jax.ShapeDtypeStruct((GP, 3 * CH + 16), BF16),
            jax.ShapeDtypeStruct((2, WIDE, 2 * HALF), BF16),
        ],
        compiler_params=params(16),
        cost_estimate=cost(2),
        name="prepare",
    )(labels, owners, counts, codebook)


def transposed_rows(half, src, rows, store):
    lane = lax.broadcasted_iota(jnp.int32, (CH, 128), 1)
    colour = lax.broadcasted_iota(jnp.int32, (CH, 128), 0) // NR

    def swapped(i):
        return jnp.swapaxes(jnp.stack([src(r, i) for r in range(NR)]).astype(F32), 0, 1)

    edge = swapped(2 * PAIRS)
    for p in range(ZP):
        parts = [swapped(half * PAIRS + ZP * c + p) for c in range(COLOUR)]
        mask = (lane // 4) == 16 * half + colour * ZP + p
        for row in rows:
            store(row, p, 0, jnp.concatenate([part[row] for part in parts], axis=0).astype(BF16))
            border = jnp.concatenate([edge[row]] * COLOUR, axis=0)
            store(row, p, 1, jnp.where(mask, border, 0.0).astype(BF16))


def normalise(value):
    mean = jnp.sum(value * value, axis=0, keepdims=True) * (1.0 / CH)
    return (value * lax.rsqrt(mean + 49.0 * NOISE_LEVEL)).astype(BF16)


def vertical(first, second, third):
    return 6.0 * second - (first + third)


def rows_at(start, size):
    return pl.ds(start if isinstance(start, int) else pl.multiple_of(start, 16), size)


def stencil_steps(half, g, bands, unit, last, xt, y, a_s, b_s):
    def regroup(k):
        base = k * 8 * STEP

        def store(row, p, t, block):
            xt[rows_at(base + (row * ZP + p) * CH, CH), t * 128 : (t + 1) * 128] = block

        transposed_rows(half, lambda r, i: g[k * NR + r, i], range(8), store)
        at = rows_at(base, 8 * STEP)
        y[at, :] = jnp.dot(xt[at, :], bands[half], preferred_element_type=F32)

    def keep():
        last[half] = xt[(ROWS - 4) * STEP :]

    def raw(row, p):
        return xt[rows_at(row * STEP + p * CH, CH), :HALF].astype(F32)

    def cols(row, p, twice):
        return y[rows_at(row * STEP + p * CH, CH), twice * HALF : (twice + 1) * HALF]

    def first(row):
        here = [raw(row, p) for p in range(ZP)]
        for p in range(ZP):
            cx = cols(row, p, 0)
            a = vertical(raw(row - 1, p), here[p], raw(row + 1, p)) - here[1 - p] - cx
            a_s[row, p] = a
            b_s[row, p] = a - cx

    def second(k):
        for odd in range(2):
            row = 2 * k + odd
            mid = [b_s[row, p] for p in range(ZP)]
            for p in range(ZP):
                mb = vertical(b_s[row - 1, p], mid[p], b_s[row + 1, p]) - mid[1 - p]
                at = (odd * ZP + p) * HALF
                unit[k, :, at : at + HALF] = normalise(a_s[row, p] + SHARPEN * (mb + cols(row, p, 1)))

    return regroup, keep, first, second


def loop(low, high, step):
    def body(k, _):
        step(k)
        return 0

    lax.fori_loop(low, high, body, 0)


def no_maximum_needed(codebook):
    wide = codebook[...].astype(F32)
    longest = jnp.max(jnp.sum(wide * wide, axis=0, keepdims=True))
    return longest * (CH * (1.01 * SOFTMAX_HEAT * LOG2E) ** 2) <= SAFE * SAFE


def posterior_steps(cbt, acc):
    slots = lax.broadcasted_iota(jnp.int32, (CELLS, VOX), 0).astype(F32).astype(BF16)

    def logits_of(u):
        stacked = jnp.concatenate([u, u, u, jnp.ones((16, VOX), BF16)], axis=0)
        return jnp.dot(cbt[...], stacked, preferred_element_type=F32)

    def add(post, label):
        onehot = jnp.where(slots == label.astype(F32).astype(BF16), jnp.ones((), BF16), jnp.zeros((), BF16))
        acc[...] += lax.dot_general(post, onehot, NT, preferred_element_type=F32)

    def begin(u, e_s):
        e = jnp.exp2(logits_of(u))
        e_s[...] = e
        return 1.0 / jnp.sum(e, axis=0, keepdims=True)

    def finish(inverse, label, e_s):
        add((e_s[...] * inverse).astype(BF16), label)

    def careful(u, label):
        logits = logits_of(u)
        e = jnp.exp2(logits - jnp.max(logits, axis=0, keepdims=True))
        add((e * (1.0 / jnp.sum(e, axis=0, keepdims=True))).astype(BF16), label)

    return begin, finish, careful


def label_row(marks, half, row):
    parts = [marks[pl.ds(p * ROWS + row + odd, 1), :] for odd in range(2) for p in range(ZP)]
    return jnp.concatenate([part[:, half * HALF : (half + 1) * HALF] for part in parts], axis=1)


def decode_kernel(g, bands, marks, cbt, codebook, acc, last, xt, y, a_s, b_s, unit0, unit1, e0, e1):
    units, buffers = (unit0, unit1), (e0, e1)
    acc[...] = jnp.zeros_like(acc)
    begin, finish, careful = posterior_steps(cbt, acc)
    halves = [stencil_steps(half, g, bands, units[half], last, xt, y, a_s, b_s) for half in range(2)]
    fine = no_maximum_needed(codebook)

    def label(half, k):
        return label_row(marks, half, 2 * k)

    def block(half, k):
        regroup, keep, first, second = halves[half]
        regroup(k)
        if k == ROWS // 8 - 1:
            keep()
        for row in range(max(8 * k - 1, 1), 8 * k + 7):
            first(row)
        pairs = list(range(max(4 * k - 1, 1), 4 * k + 3))
        for pair in pairs:
            second(pair)
        return [(half, pair) for pair in pairs]

    @pl.when(fine)
    def _():
        blocks = [(half, k) for half in range(2) for k in range(ROWS // 8)]
        ready = block(*blocks[0])
        started = None
        for number in range(len(blocks)):
            coming = block(*blocks[number + 1]) if number + 1 < len(blocks) else []
            for n, (half, pair) in enumerate(ready):
                if started is None:
                    started = (0, begin(units[half][pair], buffers[0]))
                slot, inverse = started
                following = (ready[n + 1 :] + coming)[:1]
                started = None
                for half2, pair2 in following:
                    started = (1 - slot, begin(units[half2][pair2], buffers[1 - slot]))
                finish(inverse, label(half, pair), buffers[slot])
            ready = coming

    @pl.when(jnp.logical_not(fine))
    def _():
        for half, (regroup, keep, first, second) in enumerate(halves):
            loop(0, ROWS // 8, regroup)
            keep()
            loop(1, ROWS - 1, first)
            loop(1, ROWS // 2 - 1, second)
            loop(1, ROWS // 2 - 1, lambda k: careful(units[half][k], label(half, k)))


def decode(g, bands, marks, cbt, codebook):
    return pl.pallas_call(
        decode_kernel,
        in_specs=[VMEM] * 5,
        out_specs=[VMEM] * 2,
        out_shape=[
            jax.ShapeDtypeStruct((GP, CELLS), F32),
            jax.ShapeDtypeStruct((2, 4 * STEP, WIDE), BF16),
        ],
        scratch_shapes=[
            pltpu.VMEM((ROWS * STEP, WIDE), BF16),
            pltpu.VMEM((ROWS * STEP, 2 * HALF), F32),
            pltpu.VMEM((ROWS, ZP, CH, HALF), F32),
            pltpu.VMEM((ROWS, ZP, CH, HALF), F32),
            pltpu.VMEM((ROWS // 2, CH, VOX), BF16),
            pltpu.VMEM((ROWS // 2, CH, VOX), BF16),
            pltpu.VMEM((GP, VOX), F32),
            pltpu.VMEM((GP, VOX), F32),
        ],
        compiler_params=params(36),
        cost_estimate=cost(15),
        name="decode_band",
    )(g, bands, marks, cbt, codebook)


def border_kernel(last, bands, following, marks, cbt, codebook, given, out, xh, ue, acc, e0, e1):
    joined = jnp.where(position()[0] < NZ - 1, 1.0, 0.0)

    def prepare_units():
        for half in range(2):
            xh[: 4 * STEP] = last[half]

            def store(row, p, t, block):
                start = (4 + row) * STEP + p * CH
                xh[start : start + CH, t * 128 : (t + 1) * 128] = block

            transposed_rows(half, lambda r, i: following[r * PIECE + i], range(4), store)
            y = jnp.dot(xh[STEP : 7 * STEP], bands[half], preferred_element_type=F32)

            def raw(row, p):
                return xh[row * STEP + p * CH : row * STEP + (p + 1) * CH, :HALF].astype(F32)

            def cols(row, p, twice):
                start = (row - 1) * STEP + p * CH
                return y[start : start + CH, twice * HALF : (twice + 1) * HALF]

            def up(get, row, p):
                return get(row - 1, p) * joined if row == 4 else get(row - 1, p)

            def down(get, row, p):
                return get(row + 1, p) * joined if row == 3 else get(row + 1, p)

            a, b = {}, {}
            for row in range(1, 7):
                for p in range(ZP):
                    cx = cols(row, p, 0)
                    a[row, p] = vertical(up(raw, row, p), raw(row, p), down(raw, row, p)) - raw(row, 1 - p) - cx
                    b[row, p] = a[row, p] - cx

            def get_b(row, p):
                return b[row, p]

            for row in range(2, 6):
                for p in range(ZP):
                    mb = vertical(up(get_b, row, p), b[row, p], down(get_b, row, p)) - b[row, 1 - p]
                    at = ((row % 2) * ZP + p) * HALF
                    ue[half * 2 + row // 2 - 1, :, at : at + HALF] = normalise(
                        a[row, p] + SHARPEN * (mb + cols(row, p, 1))
                    )

    acc[...] = given[...]
    tops = [following[NR * PIECE + h].astype(F32).astype(jnp.int32) for h in range(2)]

    def mark(k):
        own = [label_row(marks, h, ROWS - 2) for h in range(2)]
        next_ = [
            jnp.concatenate([tops[h][i : i + 1] for i in range(4)], axis=1) for h in range(2)
        ]
        return jnp.where(k < 2, jnp.where(k == 0, own[0], next_[0]), jnp.where(k == 2, own[1], next_[1]))

    begin, finish, careful = posterior_steps(cbt, acc)
    fine = no_maximum_needed(codebook)

    @pl.when(fine)
    def _():
        prepare_units()
        inv = begin(ue[0], e0)
        nxt = begin(ue[1], e1)
        finish(inv, mark(0), e0)
        inv = begin(ue[2], e0)
        finish(nxt, mark(1), e1)
        nxt = begin(ue[3], e1)
        finish(inv, mark(2), e0)
        finish(nxt, mark(3), e1)

    @pl.when(jnp.logical_not(fine))
    def _():
        prepare_units()
        loop(0, 4, lambda k: careful(ue[k], mark(k)))

    goes = marks[ZP * ROWS : ZP * ROWS + 1]
    select = jnp.where(lax.broadcasted_iota(jnp.int32, (TILES * CAP, CELLS), 0) == goes, SCALE, 0.0).astype(BF16)
    sums = jnp.concatenate([acc[...], jnp.zeros((128 * (FULL + 1) - GP, CELLS), F32)], axis=0)
    high = sums.astype(BF16)
    low = (sums - high.astype(F32)).astype(BF16)
    packed = lax.dot_general(select, high, NT, preferred_element_type=F32)
    packed = packed + lax.dot_general(select, low, NT, preferred_element_type=F32)
    lane = lax.broadcasted_iota(jnp.int32, (CAP // 2, 128), 1)
    for o in range(TILES):
        rows = packed[o * CAP : (o + 1) * CAP]
        for t in range(FULL):
            out[o, t * CAP : (t + 1) * CAP] = rows[:, t * 128 : (t + 1) * 128]
        rest = rows[:, FULL * 128 :]
        out[o, FULL * CAP :] = jnp.where(lane < 64, rest[: CAP // 2], pltpu.roll(rest[CAP // 2 :], 64, 1))


def border(last, bands, following, marks, cbt, codebook, given):
    return pl.pallas_call(
        border_kernel,
        in_specs=[VMEM] * 7,
        out_specs=VMEM,
        out_shape=jax.ShapeDtypeStruct((TILES, OUT_ROWS, 128), F32),
        scratch_shapes=[
            pltpu.VMEM((8 * STEP, WIDE), BF16),
            pltpu.VMEM((4, CH, VOX), BF16),
            pltpu.VMEM((GP, CELLS), F32),
            pltpu.VMEM((GP, VOX), F32),
            pltpu.VMEM((GP, VOX), F32),
        ],
        compiler_params=params(24),
        cost_estimate=cost(4),
        name="border_rows",
    )(last, bands, following, marks, cbt, codebook, given)


def unpack_kernel(parts, out):
    half_rounds = NR // 2
    y, c = lax.axis_index("y"), lax.axis_index("c")
    for other in range(2):
        for back in range(half_rounds):
            r = 2 * ((y + half_rounds - back) % half_rounds) + (c + other) % 2
            for x in range(NXD):
                src, dst = (other * half_rounds + back) * NXD + x, NXD * r + x
                for t in range(FULL):
                    out[0, dst, :, t * 128 : (t + 1) * 128] = parts[src, t * CAP : (t + 1) * CAP] * (1.0 / SCALE)
                rest = parts[src, FULL * CAP :] * (1.0 / SCALE)
                out[0, dst, : CAP // 2, FULL * 128 :] = rest[:, :REST]
                out[0, dst, CAP // 2 :, FULL * 128 :] = pltpu.roll(rest, 64, 1)[:, :REST]


def unpack(parts):
    return pl.pallas_call(
        unpack_kernel,
        in_specs=[VMEM],
        out_specs=VMEM,
        out_shape=jax.ShapeDtypeStruct((1, TILES, CAP, GENES), F32),
        compiler_params=params(16),
        name="unpack_cells",
    )(parts)


def local(images, labels, counts, owners, codebook):
    swap = [
        (z * NXD * NR + x * NR + r, r * NXD * NR + x * NR + z)
        for z in range(NZ)
        for x in range(NXD)
        for r in range(NR)
    ]
    exchange = functools.partial(lax.all_to_all, split_axis=0, concat_axis=0, tiled=True)
    g = exchange(pack(images), ("x", "y", "c"))
    marks, cbt, bands = prepare(labels, owners.reshape(1, CELLS), counts, codebook)
    marks = lax.ppermute(marks, ("z", "x", "y", "c"), swap)
    tops = marks[: ZP * ROWS].reshape(ZP, ROWS, 2, HALF)[:, :2].transpose(2, 1, 0, 3).reshape(2, 4, HALF)
    upper = jnp.concatenate([g[:NR, :, :4].reshape(NR * PIECE, 4, 128), tops.astype(BF16)], axis=0)
    following = lax.ppermute(upper, "z", [((i + 1) % NZ, i) for i in range(NZ)])
    acc, last = decode(g, bands, marks, cbt, codebook)
    packed = border(last, bands, following, marks, cbt, codebook, acc)
    parts = exchange(packed.astype(jnp.float16), ("z", "x")).reshape(NZ, NXD, OUT_ROWS, 128)
    summed = jnp.sum(parts.astype(F32), axis=0).astype(jnp.float16)
    ring = NR // 2
    order = sorted(range(1, ring), key=lambda k: -min(k, ring - k))
    sent = {k: lax.ppermute(summed, "y", [(i, (i + k) % ring) for i in range(ring)]) for k in order}
    hops = [sent[k] for k in range(1, ring)]
    own = [summed, *hops]
    others = [lax.ppermute(piece, "c", [(0, 1), (1, 0)]) for piece in own]
    received = jnp.concatenate(own + others, axis=0)
    return unpack(received.astype(F32))


def solution(mesh):
    grid = Mesh(mesh.devices.reshape(NZ, NXD, NR // 2, 2), ("z", "x", "y", "c"))
    rounds = ("y", "c")
    in_specs = (P(rounds, None, ("z", "x"), None), P(None, rounds, ("z", "x")), P(), P(("z", "x"), None), P())
    out_specs = P(("z", "x"), None, None, None)
    return jax.shard_map(local, mesh=grid, in_specs=in_specs, out_specs=out_specs, check_vma=False)
```
